256 devices in a mesh: dp: 32 (over x, z), mp: 8 (over y, core).
Axes of the slice: x: 4, y: 4, z: 8, core: 2. Of those that a mesh axis runs over, the one named last changes fastest.
Arguments:
- db_states: bfloat16 [96, 128, 8192], P('dp', 'mp'), may hold values from -6 to 6
- w_key: bfloat16 [8192, 4096], P('dp', 'mp'), may hold values from -0.0625 to 0.0625
- w_value: bfloat16 [8192, 4096], P('dp', 'mp'), may hold values from -0.0625 to 0.0625
- queries: bfloat16 [65536, 4096], P('dp', 'mp'), as said below
- nbr_owner: int32 [1024, 2], P('dp'), may hold values from 0 to 31, all different within a row; in each aligned block of 32 rows (0 to 31, 32 to 63, ...) at most 3 rows name the same one
- nbr_row: int32 [1024, 2], P('dp'), may hold values from 0 to 2
Outputs:
- attended: bfloat16 [65536, 4096], P('dp', 'mp')
The draws below stay inside these ranges and needn't reach their ends.
Inputs may be any that keep to these rules, and one draw needn't show every extreme that they name: `nbr_owner`: among the 32 segments of one index of dp, at most 3 neighbours name the same owner; the two owners of one segment differ. `queries`: outside the shown draw query rows differ in scale by up to some eight times.
All inputs are finite; a program needn't handle non-finite values.
Results may differ from the reference program's by a relative error of at most 0.025.
Values may be sent and summed in bfloat16 or wider, within the bound.
No kernel may reach another device: no remote copies, remote signals or barrier semaphores. Data moves between devices by JAX's collectives and lax.ppermute only.
A program may use at most 192 MiB of HBM per device.

```python
import math
import jax
import jax.numpy as jnp
import numpy as np
from jax import lax

D = 8192
HEADS = 32
HDIM = 128
SEGMENT = 64
NBR = 128
SEG_DEV = 32
MOST = 3
DB_DEV = 3
HD = 4096
SEGS = 1024
TOKENS = 65536
DBN = 96
N_DP = 32


def draw_queries(key, part):
    key = jax.random.fold_in(key, 11)
    first = jax.random.fold_in(key, 0)
    base = jax.random.normal(first, (TOKENS, HEADS * HDIM), jnp.float32)
    return base.astype(jnp.bfloat16)


def plant(array, stream_key, smallest, high):
    spot = [jax.random.randint(jax.random.fold_in(stream_key, axis), (), 0, length) for axis, length in enumerate(array.shape)]
    longest = array.shape.index(max(array.shape))
    neighbour = spot[:longest] + [(spot[longest] + 1) % array.shape[longest]] + spot[longest + 1:]
    return array.at[tuple(spot)].set(smallest).at[tuple(neighbour)].set(high)


def level_of(key, extent, shards, low, largest):
    loudness, own = 1.0, jax.random.fold_in(key, 6)
    for dim, parts in shards:
        steps = jnp.exp(jax.random.uniform(jax.random.fold_in(own, dim), (parts,), jnp.float32, low / len(shards), largest / len(shards)))
        loudness = loudness * jnp.repeat(steps, extent[dim] // parts).reshape([-1 if axis == dim else 1 for axis in range(len(extent))])
    return loudness


def shared_out(key, own, number, rows, number_of, top, limit, slope):
    sequence = jax.random.permutation(key, number_of)
    crowded, usual = shares(number_of, rows * top, limit, slope, True), shares(number_of, rows * top, limit, slope, False)
    places = jnp.arange(number_of)

    def named(lengths, rotation):
        used = int((lengths > 0).sum())
        fixed = max(1, used // 4)
        passed = fixed + (places - fixed + rotation * (used - fixed)) % max(1, number_of - fixed)
        return jnp.zeros((number_of,), jnp.int32).at[sequence[jnp.where(places < fixed, places, passed)]].set(jnp.asarray(lengths, jnp.int32))

    lengths = jnp.where(number % 4 == 0, named(crowded, number // 4), named(usual, number - number // 4 - 1))
    mixed = jax.random.permutation(jax.random.fold_in(own, 3), number_of)
    source_of, sink = mixed[0:number_of // 2 * 2:2], mixed[1:number_of // 2 * 2:2]
    slack = jnp.minimum(lengths[source_of] - 1, limit - lengths[sink]) // 2
    slack = jnp.where((source_of == sequence[0]) | (sink == sequence[0]) | (lengths[sink] == 0), 0, jnp.maximum(slack, 0))
    passed = jax.random.randint(jax.random.fold_in(own, 4), (number_of // 2,), 0, 1 << 20) % (slack + 1)
    lengths = lengths.at[source_of].add(-passed).at[sink].add(passed)
    labels = jnp.searchsorted(jnp.cumsum(lengths), jnp.arange(rows * top), side="right").astype(jnp.int32)
    table = labels.reshape(top, rows).T
    table = table[jax.random.permutation(jax.random.fold_in(own, 1), rows)]
    rotation = jax.random.randint(jax.random.fold_in(own, 2), (rows, 1), 0, top)
    return jnp.take_along_axis(table, (jnp.arange(top)[None, :] + rotation) % top, axis=1)


def shares(amount, total, reach, skew, full):
    loads = [(1 << 20) // math.isqrt(standing ** skew) + 1 for standing in range(1, amount + 1)]
    largest = reach if full else min(reach, max(-(-total // amount), total * loads[0] // sum(loads)))
    least = 1 if total - largest >= amount - 1 else 0
    counts, surplus = [largest] + [least] * (amount - 1), total - largest - least * (amount - 1)
    while surplus > 0:
        candidates = [i for i in range(1, amount) if counts[i] < largest] or [i for i in range(1, amount) if counts[i] < reach]
        pool, budget = sum([loads[i] for i in candidates]), surplus
        for i in candidates:
            more = min(reach - counts[i], max(1, budget * loads[i] // pool), surplus)
            counts[i] = counts[i] + more
            surplus = surplus - more
    return np.array(counts)


def centred(key, dims, scale, reach, cuts=(), dtype=jnp.bfloat16):
    values = jax.random.normal(key, dims, jnp.float32) * scale
    if len(cuts) > 0:
        values = level_of(key, dims, cuts, -0.22, 0.18) * values
    return jnp.clip(values, min=-reach, max=reach).astype(dtype)


def setup_inputs(seed: int = 0) -> dict:
    key_of = jax.random.split(jax.random.key(seed), 7)
    db_states = centred(key_of[0], (DBN, NBR, D), 1.0, 6.0, ((0, 32), (1, 8)))
    w_key = centred(key_of[1], (D, HD), D ** -0.5, 0.0625, ((0, 32), (1, 8)))
    w_value = centred(key_of[2], (D, HD), D ** -0.5, 0.0625, ((0, 32), (1, 8)))
    queries = draw_queries(jax.random.fold_in(key_of[6], 71), 0)
    nbr_owner_keys = jax.random.split(jax.random.fold_in(key_of[4], 1), SEGS // SEG_DEV)
    nbr_owner_turns = jax.random.permutation(jax.random.fold_in(key_of[4], 3), SEGS // SEG_DEV)
    nbr_owner = jax.vmap(lambda own, number: shared_out(jax.random.fold_in(key_of[4], 2), own, number, SEG_DEV, N_DP, 2, MOST, 2))(nbr_owner_keys, nbr_owner_turns).reshape((SEGS, 2))
    nbr_row = plant(jax.random.randint(key_of[5], (SEGS, 2), 0, DB_DEV), jax.random.fold_in(key_of[5], 1), 0, DB_DEV - 1).astype(jnp.int32)
    return dict(db_states=db_states, w_key=w_key, w_value=w_value, queries=queries, nbr_owner=nbr_owner, nbr_row=nbr_row)


def attend(query, key_rows, value_rows):
    score = jnp.einsum('qhd,khd->hqk', query.astype(jnp.float32), key_rows.astype(jnp.float32)) * (HDIM ** -0.5)
    maxima = jnp.max(score, axis=-1)
    weights = jnp.exp(score - maxima[..., None])
    totals = jnp.sum(weights, axis=-1)
    partial_out = jnp.einsum('hqk,khd->qhd', weights, value_rows.astype(jnp.float32)).astype(jnp.bfloat16)
    return partial_out, maxima, totals


def reference(db_states, w_key, w_value, queries, nbr_owner, nbr_row):
    flattened = db_states.reshape(-1, D)
    keys = jnp.dot(flattened, w_key, preferred_element_type=jnp.float32).astype(jnp.bfloat16).reshape(-1, NBR, HEADS, HDIM)
    values = jnp.dot(flattened, w_value, preferred_element_type=jnp.float32).astype(jnp.bfloat16).reshape(-1, NBR, HEADS, HDIM)
    entry = (nbr_owner * DB_DEV + nbr_row).astype(jnp.int32)
    grouped = queries.reshape(-1, SEGMENT, HEADS, HDIM)

    def one_segment(inputs):
        query, picks = inputs
        first = attend(query, keys[picks[0]], values[picks[0]])
        second = attend(query, keys[picks[1]], values[picks[1]])
        highest = jnp.maximum(first[1], second[1])
        weight_a = jnp.exp(first[1] - highest)
        weight_b = jnp.exp(second[1] - highest)
        numer = first[0].astype(jnp.float32) * weight_a.T[:, :, None] + second[0].astype(jnp.float32) * weight_b.T[:, :, None]
        denom = first[2] * weight_a + second[2] * weight_b
        return (numer / denom.T[:, :, None]).reshape(SEGMENT, HEADS * HDIM).astype(jnp.bfloat16)

    result = lax.map(one_segment, (grouped, entry))
    return result.reshape(-1, HEADS * HDIM)
```

```python
import functools

import jax
import jax.numpy as jnp
from jax import lax
from jax.experimental import pallas as pl
from jax.experimental.pallas import tpu as pltpu
from jax.sharding import PartitionSpec as P

HDIM = 128
SEGMENT = 64
XN, ZN = 4, 8
HELD = 3
TOK = 64
CHUNK_HEADS = 2
BF = jnp.bfloat16
F32 = jnp.float32


def moved(array, to):
    pairs = []
    for x in range(XN):
        for z in range(ZN):
            tx, tz = to(x, z)
            pairs.append((x * ZN + z, (tx % XN) * ZN + tz % ZN))
    return lax.ppermute(array, "dp", pairs)


def up(array):
    return moved(array, lambda x, z: (x, z + 1))


def down(array):
    return moved(array, lambda x, z: (x, z - 1))


def cross(array):
    return moved(array, lambda x, z: (x ^ 3, z))


def pair(array):
    return moved(array, lambda x, z: (x ^ 1, z))


def gather16(a, b):
    rows = a.shape[0]
    half = rows // 2
    join = functools.partial(jnp.concatenate, axis=0)
    up1, down1, other_a = up(b), down(b), cross(a)
    up2 = up(join([a, other_a, up1]))
    down2 = down(join([other_a, a, down1]))
    side2 = cross(join([b, up1, down1]))
    up3, down3 = up(up2), down(down2)
    side3 = cross(join([up2[2 * rows :], down2[2 * rows :]]))
    up4 = up(up3[: 2 * rows + half])
    down4 = down(join([down3[: 2 * rows], down3[2 * rows + half :]]))
    side4 = cross(join([up3[2 * rows :], down3[2 * rows :]]))
    up5, down5 = up(up4[:rows]), down(down4[:rows])
    side5 = cross(join([up4[2 * rows :], down4[2 * rows :]]))
    arrays = [a, b, other_a, up1, down1, up2, down2, side2, up3, down3, side3, up4, down4, side4, up5, down5, side5]
    pieces = [
        (0, 0, rows, 0, 0, 0),
        (1, 0, rows, 1, 0, 0),
        (2, 0, rows, 0, 8, 0),
        (3, 0, rows, 1, 1, 0),
        (4, 0, rows, 1, 7, 0),
        (7, 0, rows, 1, 8, 0),
        (7, rows, rows, 1, 9, 0),
        (7, 2 * rows, rows, 1, 15, 0),
        (10, 0, rows, 1, 10, 0),
        (10, rows, rows, 1, 14, 0),
        (13, 0, rows, 1, 11, 0),
        (13, rows, rows, 1, 13, 0),
        (14, 0, rows, 0, 4, 0),
        (15, 0, rows, 0, 12, 0),
        (16, 0, rows, 1, 12, 0),
        (11, 2 * rows, half, 1, 4, 0),
        (12, 2 * rows, half, 1, 4, half),
        (5, 2 * rows, rows, 1, 2, 0),
        (6, 2 * rows, rows, 1, 6, 0),
        (8, 2 * rows, rows, 1, 3, 0),
        (9, 2 * rows, rows, 1, 5, 0),
    ]
    for step, array in ((1, 5), (2, 8), (3, 11)):
        pieces += [(array, 0, rows, 0, step, 0), (array, rows, rows, 0, 8 + step, 0)]
    for step, array in ((1, 6), (2, 9), (3, 12)):
        pieces += [(array, 0, rows, 0, 16 - step, 0), (array, rows, rows, 0, 8 - step, 0)]
    return arrays, pieces


ROW_TILE = 192


def project_kernel(pieces, place_ref, half_ref, db_hbm, *refs):
    count = 17
    w_refs = refs[:count]
    mine_k, mine_v, send_k, send_v, db_ref, w_ref, db_sem, w_sem = refs[count:]
    db_copy = pltpu.make_async_copy(db_hbm, db_ref, db_sem)
    db_copy.start()
    copies = []
    for i, (array, first, rows, kind, place, at) in enumerate(pieces):
        copies.append(
            pltpu.make_async_copy(
                w_refs[array].at[pl.ds(first, rows)],
                w_ref.at[kind, place_ref[place], pl.ds(at, rows)],
                w_sem.at[i],
            )
        )
        copies[-1].start()
    db_copy.wait()
    for copy in copies:
        copy.wait()
    depth = w_ref.shape[1] * w_ref.shape[2]
    width = w_ref.shape[3]
    blocks = db_ref.shape[0] // 2 // 16
    per_tile = ROW_TILE // 16
    entries = 2 * HELD
    for own in (0, 1):
        side = half_ref[0] if own else 1 - half_ref[0]
        for tile in range(blocks // per_tile):
            start = pl.multiple_of(side * (blocks * 16) + tile * ROW_TILE, ROW_TILE)
            rows = db_ref[pl.ds(start, ROW_TILE), :]
            for kind in (0, 1):
                part = jnp.dot(rows, w_ref[kind].reshape(depth, width), preferred_element_type=F32)
                for j in range(per_tile):
                    group, entry = divmod(tile * per_tile + j, entries)
                    target = entry * TOK + group * 16
                    piece = part[j * 16 : (j + 1) * 16]
                    if own:
                        (mine_v if kind else mine_k)[target : target + 16, :] = piece
                    else:
                        (send_v if kind else send_k)[target : target + 16, :] = piece.astype(BF)


def project(db, arrays, pieces, places, side):
    rows, depth = db.shape
    width = arrays[0].shape[1]
    half = rows // 2
    vmem = pl.BlockSpec(memory_space=pltpu.VMEM)
    anywhere = pl.BlockSpec(memory_space=pl.ANY)
    smem = pl.BlockSpec(memory_space=pltpu.SMEM)
    return pl.pallas_call(
        functools.partial(project_kernel, pieces),
        out_shape=[jax.ShapeDtypeStruct((half, width), F32)] * 2 + [jax.ShapeDtypeStruct((half, width), BF)] * 2,
        in_specs=[smem, smem] + [anywhere] * (1 + len(arrays)),
        out_specs=[vmem] * 4,
        scratch_shapes=[
            pltpu.VMEM((rows, depth), BF),
            pltpu.VMEM((2, 16, depth // 16, width), BF),
            pltpu.SemaphoreType.DMA,
            pltpu.SemaphoreType.DMA((len(pieces),)),
        ],
        compiler_params=pltpu.CompilerParams(vmem_limit_bytes=48 << 20),
        cost_estimate=pl.CostEstimate(flops=4 * rows * depth * width, bytes_accessed=24 << 20, transcendentals=0),
        name="project",
    )(places, side, db, *arrays)


def attend_kernel(pieces, first_head, slot_ref, q_ref, *refs):
    count = 17
    kv_refs = refs[:count]
    out_ref, stat_ref, kv_ref, sem = refs[count:]
    copies = []
    for i, (array, first, rows, kind, place, at) in enumerate(pieces):
        copies.append(
            pltpu.make_async_copy(
                kv_refs[array].at[pl.ds(first, rows)],
                kv_ref.at[kind, pl.ds(place * 6 * TOK + at, rows)],
                sem.at[i],
            )
        )
        copies[-1].start()
    for copy in copies:
        copy.wait()
    stat_ref[...] = jnp.zeros_like(stat_ref)
    lane = lax.broadcasted_iota(jnp.int32, (SEGMENT, 128), 1)
    heads = q_ref.shape[1] // HDIM

    def unit(u, carry):
        at = pl.multiple_of(u * SEGMENT, SEGMENT)
        one = pl.multiple_of(slot_ref[2 * u] * TOK, TOK)
        two = pl.multiple_of(slot_ref[2 * u + 1] * TOK, TOK)
        stat = stat_ref[...]
        for j in range(heads):
            cols = slice(j * HDIM, (j + 1) * HDIM)
            q = q_ref[pl.ds(at, SEGMENT), cols]
            keys = jnp.concatenate([kv_ref[0, pl.ds(one, TOK), cols], kv_ref[0, pl.ds(two, TOK), cols]], axis=0)
            values = jnp.concatenate([kv_ref[1, pl.ds(one, TOK), cols], kv_ref[1, pl.ds(two, TOK), cols]], axis=0)
            score = lax.dot_general(q, keys, (((1,), (1,)), ((), ())), preferred_element_type=F32) * (HDIM**-0.5)
            top = jnp.max(score, axis=1, keepdims=True)
            weight = jnp.exp(score - top)
            total = jnp.sum(weight, axis=1, keepdims=True)
            mixed = jnp.dot(weight.astype(BF), values, preferred_element_type=F32)
            out_ref[pl.ds(at, SEGMENT), cols] = (mixed / total).astype(BF)
            stat = jnp.where(lane == u * heads + j, top + jnp.log(total), stat)
        stat_ref[...] = stat
        return carry

    lax.fori_loop(0, q_ref.shape[0] // SEGMENT, unit, 0, unroll=4)


def attend(slots, queries, chunk, arrays, pieces):
    rows = queries.shape[0]
    width = arrays[0].shape[1]
    block = arrays[0].shape[0]
    smem = pl.BlockSpec(memory_space=pltpu.SMEM)
    anywhere = pl.BlockSpec(memory_space=pl.ANY)
    return pl.pallas_call(
        functools.partial(attend_kernel, pieces, chunk * CHUNK_HEADS),
        grid=(1,),
        out_shape=[jax.ShapeDtypeStruct((rows, width), BF), jax.ShapeDtypeStruct((SEGMENT, 128), F32)],
        in_specs=[smem, pl.BlockSpec((rows, width), lambda i: (0, chunk))] + [anywhere] * len(arrays),
        out_specs=[pl.BlockSpec((rows, width), lambda i: (0, 0)), pl.BlockSpec((SEGMENT, 128), lambda i: (0, 0))],
        scratch_shapes=[pltpu.VMEM((2, 16 * block, width), BF), pltpu.SemaphoreType.DMA((len(pieces),))],
        compiler_params=pltpu.CompilerParams(vmem_limit_bytes=40 << 20),
        cost_estimate=pl.CostEstimate(flops=4 * rows * 128 * width, bytes_accessed=10 << 20, transcendentals=rows * width),
        name="attend",
    )(slots, queries, *arrays)


def merge_kernel(mine_ref, theirs_ref, stat_ref, other_ref, *refs):
    out_ref = refs[-1]
    lane = lax.broadcasted_iota(jnp.int32, (SEGMENT, 128), 1)
    heads = mine_ref.shape[1] // HDIM
    difference = other_ref[...] - stat_ref[...]

    def unit(u, carry):
        at = pl.multiple_of(u * SEGMENT, SEGMENT)
        for j in range(heads):
            cols = slice(j * HDIM, (j + 1) * HDIM)
            gap = jnp.sum(jnp.where(lane == u * heads + j, difference, 0.0), axis=1, keepdims=True)
            small = jnp.exp(-jnp.abs(gap))
            larger = 1.0 / (1.0 + small)
            smaller = small * larger
            share = jnp.where(gap > 0, smaller, larger)
            rest = jnp.where(gap > 0, larger, smaller)
            a = mine_ref[pl.ds(at, SEGMENT), cols].astype(F32)
            b = theirs_ref[pl.ds(at, SEGMENT), cols].astype(F32)
            out_ref[pl.ds(at, SEGMENT), cols] = (a * share + b * rest).astype(BF)
        return carry

    lax.fori_loop(0, mine_ref.shape[0] // SEGMENT, unit, 0, unroll=4)


def merge(mine, theirs, stat, other, chunk, full_width, so_far):
    rows, width = mine.shape
    whole = pl.BlockSpec((rows, width), lambda i: (0, 0))
    stats = pl.BlockSpec((SEGMENT, 128), lambda i: (0, 0))
    extra = [] if so_far is None else [so_far]
    return pl.pallas_call(
        merge_kernel,
        grid=(1,),
        out_shape=jax.ShapeDtypeStruct((rows, full_width), BF),
        in_specs=[whole, whole, stats, stats] + [pl.BlockSpec(memory_space=pl.ANY)] * len(extra),
        out_specs=pl.BlockSpec((rows, width), lambda i: (0, chunk)),
        input_output_aliases={4: 0} if extra else {},
        compiler_params=pltpu.CompilerParams(vmem_limit_bytes=32 << 20),
        cost_estimate=pl.CostEstimate(flops=8 * rows * width, bytes_accessed=6 * rows * width, transcendentals=rows),
        name="merge",
    )(mine, theirs, stat, other, *extra)


def local(db_states, w_key, w_value, queries, nbr_owner, nbr_row):
    place = lax.axis_index("dp")
    x, z = place // ZN, place % ZN
    side = ((x + 1) // 2) % 2
    quarter = db_states.shape[2] // XN

    outer = jnp.concatenate([db_states[..., :quarter], db_states[..., 3 * quarter :]], axis=-1)
    inner = db_states[..., quarter : 3 * quarter]
    kept = jnp.where(side == 0, outer, inner)
    given = pair(jnp.where(side == 0, inner, outer))
    even = x % 2 == 0
    six = jnp.concatenate([jnp.where(even, kept, given), jnp.where(even, given, kept)], axis=0)
    db = lax.all_gather(six, "mp", axis=0, tiled=False).reshape(-1, 2 * quarter)

    w_arrays, w_pieces = gather16(w_key, w_value)
    their_queries = pair(queries)
    tables = pair(jnp.concatenate([nbr_owner, nbr_row], axis=1))

    k = jnp.arange(ZN)
    near = (z - k) % ZN + jnp.where(x >= 2, ZN, 0)
    far = (z - k) % ZN + jnp.where(x >= 2, 0, ZN)
    places = jnp.concatenate([near, far]).astype(jnp.int32)
    mine_k, mine_v, send_k, send_v = project(db, w_arrays, w_pieces, places, side.reshape(1).astype(jnp.int32))

    def slots(owner, row):
        from_x, from_z = owner // ZN, owner % ZN
        block = jnp.where(from_x // 2 == x // 2, 0, ZN) + (z - from_z) % ZN
        return (block * (2 * HELD) + (from_x % 2) * HELD + row).reshape(-1).astype(jnp.int32)

    own_slots = slots(nbr_owner, nbr_row)
    their_slots = slots(tables[:, :2], tables[:, 2:])

    width = CHUNK_HEADS * HDIM
    columns = queries.shape[1]
    output = None
    for chunk in range(columns // width):
        cols = slice(chunk * width, (chunk + 1) * width)
        got = pair(jnp.concatenate([send_k[:, cols], send_v[:, cols]], axis=0))
        half = got.shape[0] // 2
        keys = (mine_k[:, cols] + got[:half].astype(F32)).astype(BF)
        values = (mine_v[:, cols] + got[half:].astype(F32)).astype(BF)
        arrays, pieces = gather16(keys, values)
        given, given_stat = attend(their_slots, their_queries, chunk, arrays, pieces)
        theirs, other = pair(given), pair(given_stat)
        mine, stat = attend(own_slots, queries, chunk, arrays, pieces)
        output = merge(mine, theirs, stat, other, chunk, columns, output)
    return output


def solution(mesh):
    in_specs = (
        P("dp", "mp", None),
        P("dp", "mp"),
        P("dp", "mp"),
        P("dp", "mp"),
        P("dp", None),
        P("dp", None),
    )
    out_specs = P("dp", "mp")
    return jax.shard_map(local, mesh=mesh, in_specs=in_specs, out_specs=out_specs, check_vma=False)
```

```python
import functools

import jax
import jax.numpy as jnp
from jax import lax
from jax.experimental import pallas as pl
from jax.experimental.pallas import tpu as pltpu
from jax.sharding import PartitionSpec as P

HDIM = 128
SEGMENT = 64
XN, ZN = 4, 8
HELD = 3
TOK = 64
CHUNK_HEADS = 2
BF = jnp.bfloat16
F32 = jnp.float32


def moved(array, to):
    pairs = []
    for x in range(XN):
        for z in range(ZN):
            tx, tz = to(x, z)
            pairs.append((x * ZN + z, (tx % XN) * ZN + tz % ZN))
    return lax.ppermute(array, "dp", pairs)


def up(array):
    return moved(array, lambda x, z: (x, z + 1))


def down(array):
    return moved(array, lambda x, z: (x, z - 1))


def cross(array):
    return moved(array, lambda x, z: (x ^ 3, z))


def pair(array):
    return moved(array, lambda x, z: (x ^ 1, z))


def gather16(a, b):
    rows = a.shape[0]
    half = rows // 2
    join = functools.partial(jnp.concatenate, axis=0)
    up1, down1, other_a = yield [up(b), down(b), cross(a)]
    up2, down2, side2 = yield [up(join([a, other_a, up1])), down(join([other_a, a, down1])), cross(join([b, up1, down1]))]
    up3, down3, side3 = yield [up(up2), down(down2), cross(join([up2[2 * rows :], down2[2 * rows :]]))]
    up4, down4, side4 = yield [
        up(up3[: 2 * rows + half]),
        down(join([down3[: 2 * rows], down3[2 * rows + half :]])),
        cross(join([up3[2 * rows :], down3[2 * rows :]])),
    ]
    up5, down5, side5 = yield [up(up4[:rows]), down(down4[:rows]), cross(join([up4[2 * rows :], down4[2 * rows :]]))]
    arrays = [a, b, other_a, up1, down1, up2, down2, side2, up3, down3, side3, up4, down4, side4, up5, down5, side5]
    return arrays, pieces_of(rows)


def pieces_of(rows):
    half = rows // 2
    pieces = [
        (0, 0, rows, 0, 0, 0),
        (1, 0, rows, 1, 0, 0),
        (2, 0, rows, 0, 8, 0),
        (3, 0, rows, 1, 1, 0),
        (4, 0, rows, 1, 7, 0),
        (7, 0, rows, 1, 8, 0),
        (7, rows, rows, 1, 9, 0),
        (7, 2 * rows, rows, 1, 15, 0),
        (10, 0, rows, 1, 10, 0),
        (10, rows, rows, 1, 14, 0),
        (13, 0, rows, 1, 11, 0),
        (13, rows, rows, 1, 13, 0),
        (14, 0, rows, 0, 4, 0),
        (15, 0, rows, 0, 12, 0),
        (16, 0, rows, 1, 12, 0),
        (11, 2 * rows, half, 1, 4, 0),
        (12, 2 * rows, half, 1, 4, half),
        (5, 2 * rows, rows, 1, 2, 0),
        (6, 2 * rows, rows, 1, 6, 0),
        (8, 2 * rows, rows, 1, 3, 0),
        (9, 2 * rows, rows, 1, 5, 0),
    ]
    for step, array in ((1, 5), (2, 8), (3, 11)):
        pieces += [(array, 0, rows, 0, step, 0), (array, rows, rows, 0, 8 + step, 0)]
    for step, array in ((1, 6), (2, 9), (3, 12)):
        pieces += [(array, 0, rows, 0, 16 - step, 0), (array, rows, rows, 0, 8 - step, 0)]
    return pieces


def rounds(*parts):
    results, live, sent, now = [None] * len(parts), {}, {}, 0
    while None in results:
        for i, (first, part) in enumerate(parts):
            if first == now:
                live[i] = part
        batch = {}
        for i in list(live):
            try:
                batch[i] = live[i].send(sent.get(i))
            except StopIteration as end:
                results[i] = end.value
                del live[i]
        flat = lax.optimization_barrier([array for group in batch.values() for array in group])
        for i, group in batch.items():
            sent[i], flat = flat[: len(group)], flat[len(group) :]
        now += 1
    return results


ROW_TILE = 192


def project_kernel(pieces, first_col, place_ref, half_ref, db_hbm, *refs):
    count = 17
    w_refs = refs[:count]
    mine_k, mine_v, send_ref, db_ref, w_ref, db_sem, w_sem = refs[count:]
    width = w_ref.shape[3]
    db_copy = pltpu.make_async_copy(db_hbm, db_ref, db_sem)
    db_copy.start()
    copies = []
    for i, (array, first, rows, kind, place, at) in enumerate(pieces):
        copies.append(
            pltpu.make_async_copy(
                w_refs[array].at[pl.ds(first, rows), pl.ds(first_col, width)],
                w_ref.at[kind, place_ref[place], pl.ds(at, rows)],
                w_sem.at[i],
            )
        )
        copies[-1].start()
    db_copy.wait()
    for copy in copies:
        copy.wait()
    depth = w_ref.shape[1] * w_ref.shape[2]
    blocks = db_ref.shape[0] // 2 // 16
    per_tile = ROW_TILE // 16
    entries = 2 * HELD
    for own in (0, 1):
        side = half_ref[0] if own else 1 - half_ref[0]
        for tile in range(blocks // per_tile):
            start = pl.multiple_of(side * (blocks * 16) + tile * ROW_TILE, ROW_TILE)
            rows = db_ref[pl.ds(start, ROW_TILE), :]
            for kind in (0, 1):
                part = jnp.dot(rows, w_ref[kind].reshape(depth, width), preferred_element_type=F32)
                for j in range(per_tile):
                    group, entry = divmod(tile * per_tile + j, entries)
                    target = entry * TOK + group * 16
                    piece = part[j * 16 : (j + 1) * 16]
                    if own:
                        (mine_v if kind else mine_k)[target : target + 16, :] = piece
                    else:
                        send_ref[kind, target : target + 16, :] = piece.astype(BF)


def project(db, arrays, pieces, places, side, chunk):
    rows, depth = db.shape
    width = CHUNK_HEADS * HDIM
    half = rows // 2
    vmem = pl.BlockSpec(memory_space=pltpu.VMEM)
    anywhere = pl.BlockSpec(memory_space=pl.ANY)
    smem = pl.BlockSpec(memory_space=pltpu.SMEM)
    return pl.pallas_call(
        functools.partial(project_kernel, pieces, chunk * width),
        out_shape=[jax.ShapeDtypeStruct((half, width), F32)] * 2 + [jax.ShapeDtypeStruct((2, half, width), BF)],
        in_specs=[smem, smem] + [anywhere] * (1 + len(arrays)),
        out_specs=[vmem] * 3,
        scratch_shapes=[
            pltpu.VMEM((rows, depth), BF),
            pltpu.VMEM((2, 16, depth // 16, width), BF),
            pltpu.SemaphoreType.DMA,
            pltpu.SemaphoreType.DMA((len(pieces),)),
        ],
        compiler_params=pltpu.CompilerParams(vmem_limit_bytes=60 << 20),
        cost_estimate=pl.CostEstimate(flops=4 * rows * depth * width, bytes_accessed=16 << 20, transcendentals=0),
        name="project",
    )(places, side, db, *arrays)


GROUP = 8


def attend_kernel(pieces, first_col, slot_ref, own_hbm, *refs):
    count = 17
    q_parts = refs[:4]
    kv_refs = refs[4 : 4 + count]
    given_ref, mine_ref, given_stat, mine_stat, q_ref, kv_ref, q_sem, sem = refs[4 + count :]
    width = kv_ref.shape[2]
    copies = []
    part = q_parts[0].shape[0]
    sources = [(q, i * part) for i, q in enumerate(q_parts)] + [(own_hbm, 4 * part)]
    for i, (source, at) in enumerate(sources):
        rows = source.shape[0]
        copies.append(
            pltpu.make_async_copy(source.at[:, pl.ds(first_col, width)], q_ref.at[pl.ds(at, rows)], q_sem.at[i])
        )
        copies[-1].start()
    for i, (array, first, rows, kind, place, at) in enumerate(pieces):
        copies.append(
            pltpu.make_async_copy(
                kv_refs[array].at[pl.ds(first, rows)],
                kv_ref.at[kind, pl.ds(place * 6 * TOK + at, rows)],
                sem.at[i],
            )
        )
        copies[-1].start()
    for copy in copies:
        copy.wait()
    lane = lax.broadcasted_iota(jnp.int32, (SEGMENT, 128), 1)
    heads = width // HDIM
    segments = q_ref.shape[0] // SEGMENT // 2

    for base, out_ref, stat_ref in ((0, given_ref, given_stat), (segments, mine_ref, mine_stat)):

        def group(g, stat, base=base, out_ref=out_ref):
            tasks, scores, results = [], [], []
            for i in range(GROUP):
                u = g * GROUP + i
                at = pl.multiple_of(u * SEGMENT, SEGMENT)
                one = pl.multiple_of(slot_ref[2 * (base + u)] * TOK, TOK)
                two = pl.multiple_of(slot_ref[2 * (base + u) + 1] * TOK, TOK)
                for j in range(heads):
                    tasks.append((u, at, one, two, j, slice(j * HDIM, (j + 1) * HDIM)))
            for u, at, one, two, j, cols in tasks:
                q = q_ref[pl.ds(base * SEGMENT + at, SEGMENT), cols]
                keys = jnp.concatenate([kv_ref[0, pl.ds(one, TOK), cols], kv_ref[0, pl.ds(two, TOK), cols]], axis=0)
                score = lax.dot_general(q, keys, (((1,), (1,)), ((), ())), preferred_element_type=F32)
                scores.append(score * (HDIM**-0.5))
            tops = [jnp.max(score, axis=1, keepdims=True) for score in scores]
            weights = [jnp.exp(score - top) for score, top in zip(scores, tops)]
            for (u, at, one, two, j, cols), weight in zip(tasks, weights):
                values = jnp.concatenate([kv_ref[1, pl.ds(one, TOK), cols], kv_ref[1, pl.ds(two, TOK), cols]], axis=0)
                mixed = jnp.dot(weight.astype(BF), values, preferred_element_type=F32)
                results.append((mixed, jnp.sum(weight, axis=1, keepdims=True)))
            for (u, at, one, two, j, cols), (mixed, total), top in zip(tasks, results, tops):
                out_ref[pl.ds(at, SEGMENT), cols] = (mixed / total).astype(BF)
                stat = jnp.where(lane == u * heads + j, top + jnp.log(total), stat)
            return stat

        stat_ref[...] = lax.fori_loop(0, segments // GROUP, group, jnp.zeros((SEGMENT, 128), F32))


def attend(slots, queries, their_parts, chunk, arrays, pieces):
    rows = queries.shape[0]
    block, width = arrays[0].shape
    smem = pl.BlockSpec(memory_space=pltpu.SMEM)
    vmem = pl.BlockSpec(memory_space=pltpu.VMEM)
    anywhere = pl.BlockSpec(memory_space=pl.ANY)
    return pl.pallas_call(
        functools.partial(attend_kernel, pieces, chunk * width),
        out_shape=[jax.ShapeDtypeStruct((rows, width), BF)] * 2 + [jax.ShapeDtypeStruct((SEGMENT, 128), F32)] * 2,
        in_specs=[smem] + [anywhere] * (1 + len(their_parts) + len(arrays)),
        out_specs=[vmem] * 4,
        scratch_shapes=[
            pltpu.VMEM((2 * rows, width), BF),
            pltpu.VMEM((2, 16 * block, width), BF),
            pltpu.SemaphoreType.DMA((len(their_parts) + 1,)),
            pltpu.SemaphoreType.DMA((len(pieces),)),
        ],
        compiler_params=pltpu.CompilerParams(vmem_limit_bytes=60 << 20),
        cost_estimate=pl.CostEstimate(flops=8 * rows * 128 * width, bytes_accessed=12 << 20, transcendentals=rows * width),
        name="attend",
    )(slots, queries, *their_parts, *arrays)


def merge_kernel(mine_ref, theirs_ref, stat_ref, other_ref, *refs):
    out_ref = refs[-1]
    lane = lax.broadcasted_iota(jnp.int32, (SEGMENT, 128), 1)
    heads = mine_ref.shape[1] // HDIM
    difference = other_ref[...] - stat_ref[...]

    def unit(u, carry):
        at = pl.multiple_of(u * SEGMENT, SEGMENT)
        for j in range(heads):
            cols = slice(j * HDIM, (j + 1) * HDIM)
            gap = jnp.sum(jnp.where(lane == u * heads + j, difference, 0.0), axis=1, keepdims=True)
            small = jnp.exp(-jnp.abs(gap))
            larger = 1.0 / (1.0 + small)
            smaller = small * larger
            share = jnp.where(gap > 0, smaller, larger)
            rest = jnp.where(gap > 0, larger, smaller)
            a = mine_ref[pl.ds(at, SEGMENT), cols].astype(F32)
            b = theirs_ref[pl.ds(at, SEGMENT), cols].astype(F32)
            out_ref[pl.ds(at, SEGMENT), cols] = (a * share + b * rest).astype(BF)
        return carry

    lax.fori_loop(0, mine_ref.shape[0] // SEGMENT, unit, 0, unroll=4)


def merge(mine, theirs, stat, other, chunk, full_width, so_far):
    rows, width = mine.shape
    whole = pl.BlockSpec((rows, width), lambda i: (0, 0))
    stats = pl.BlockSpec((SEGMENT, 128), lambda i: (0, 0))
    extra = [] if so_far is None else [so_far]
    return pl.pallas_call(
        merge_kernel,
        grid=(1,),
        out_shape=jax.ShapeDtypeStruct((rows, full_width), BF),
        in_specs=[whole, whole, stats, stats] + [pl.BlockSpec(memory_space=pl.ANY)] * len(extra),
        out_specs=pl.BlockSpec((rows, width), lambda i: (0, chunk)),
        input_output_aliases={4: 0} if extra else {},
        compiler_params=pltpu.CompilerParams(vmem_limit_bytes=12 << 20),
        cost_estimate=pl.CostEstimate(flops=8 * rows * width, bytes_accessed=6 * rows * width, transcendentals=rows),
        name="merge",
    )(mine, theirs, stat, other, *extra)


def local(db_states, w_key, w_value, queries, nbr_owner, nbr_row):
    place = lax.axis_index("dp")
    x, z = place // ZN, place % ZN
    side = ((x + 1) // 2) % 2
    quarter = db_states.shape[2] // XN
    rows, columns = queries.shape

    outer = jnp.concatenate([db_states[..., :quarter], db_states[..., 3 * quarter :]], axis=-1)
    inner = db_states[..., quarter : 3 * quarter]
    kept = jnp.where(side == 0, outer, inner)
    given = jnp.where(side == 0, inner, outer)
    even = x % 2 == 0

    def pair_traffic():
        got, tables = yield [pair(given), pair(jnp.concatenate([nbr_owner, nbr_row], axis=1))]
        six = jnp.concatenate([jnp.where(even, kept, got), jnp.where(even, got, kept)], axis=0)
        db = lax.all_gather(six, "mp", axis=0, tiled=False).reshape(-1, 2 * quarter)
        parts, step = [], rows // 4
        for i in range(4):
            parts += yield [pair(queries[i * step : (i + 1) * step])]
        return db, tables, parts

    (w_arrays, w_pieces), (db, tables, their_parts) = rounds((0, gather16(w_key, w_value)), (0, pair_traffic()))

    k = jnp.arange(ZN)
    near = (z - k) % ZN + jnp.where(x >= 2, ZN, 0)
    far = (z - k) % ZN + jnp.where(x >= 2, 0, ZN)
    places = jnp.concatenate([near, far]).astype(jnp.int32)

    def slots(owner, row):
        from_x, from_z = owner // ZN, owner % ZN
        block = jnp.where(from_x // 2 == x // 2, 0, ZN) + (z - from_z) % ZN
        return (block * (2 * HELD) + (from_x % 2) * HELD + row).reshape(-1).astype(jnp.int32)

    all_slots = jnp.concatenate([slots(tables[:, :2], tables[:, 2:]), slots(nbr_owner, nbr_row)])
    flag = side.reshape(1).astype(jnp.int32)
    mine_k0, mine_v0, send0 = project(db, w_arrays, w_pieces, places, flag, 0)
    mine_k1, mine_v1, send1 = project(db, w_arrays, w_pieces, places, flag, 1)
    got0 = pair(send0)

    def summed(mine, got):
        return (mine + got.astype(F32)).astype(BF)

    def second():
        (got1,) = yield [pair(send1)]
        for _ in range(3):
            yield []
        return (yield from gather16(summed(mine_k1, got1[0]), summed(mine_v1, got1[1])))

    def output_of_first(answer):
        step = rows // 2
        parts, stat = [], None
        yield []
        first, stat = yield [pair(answer[0][:step]), pair(answer[2])]
        (last,) = yield [pair(answer[0][step:])]
        return jnp.concatenate([first, last], axis=0), stat

    first = gather16(summed(mine_k0, got0[0]), summed(mine_v0, got0[1]))
    holder = {}

    def third():
        answer = attend(all_slots, queries, their_parts, 0, *holder["kv"])
        holder["answer"] = answer
        return (yield from output_of_first(answer))

    def kept_first():
        holder["kv"] = yield from first
        return holder["kv"]

    _, (arrays1, pieces1), (theirs0, other0) = rounds((0, kept_first()), (0, second()), (5, third()))
    answer0 = holder["answer"]
    output = merge(answer0[1], theirs0, answer0[3], other0, 0, columns, None)
    answer1 = attend(all_slots, queries, their_parts, 1, arrays1, pieces1)
    theirs1, other1 = pair(answer1[0]), pair(answer1[2])
    return merge(answer1[1], theirs1, answer1[3], other1, 1, columns, output)


def solution(mesh):
    in_specs = (
        P("dp", "mp", None),
        P("dp", "mp"),
        P("dp", "mp"),
        P("dp", "mp"),
        P("dp", None),
        P("dp", None),
    )
    out_specs = P("dp", "mp")
    return jax.shard_map(local, mesh=mesh, in_specs=in_specs, out_specs=out_specs, check_vma=False)
```

```python
import functools

import jax
import jax.numpy as jnp
from jax import lax
from jax.experimental import pallas as pl
from jax.experimental.pallas import tpu as pltpu
from jax.sharding import PartitionSpec as P

HDIM = 128
SEGMENT = 64
XN, ZN = 4, 8
HELD = 3
TOK = 64
CHUNKS = ((0, 2), (2, 2))
BF = jnp.bfloat16
F32 = jnp.float32


WAYS = {
    "up": lambda x, z: (x, z + 1),
    "down": lambda x, z: (x, z - 1),
    "cross": lambda x, z: (x ^ 3, z),
    "pair": lambda x, z: (x ^ 1, z),
    "diagonal": lambda x, z: (x ^ 2, z),
}


def move(way, array):
    pairs = []
    for x in range(XN):
        for z in range(ZN):
            tx, tz = WAYS[way](x, z)
            pairs.append((x * ZN + z, tx * ZN + tz % ZN))
    return lax.ppermute(array, "dp", pairs)


def up(array):
    return "up", array


def down(array):
    return "down", array


def cross(array):
    return "cross", array


def pair(array):
    return "pair", array


def diagonal(array):
    return "diagonal", array


def stay(array):
    return "stay", array


def sent(messages):
    together = {}
    for i, (way, array) in enumerate(messages):
        key = (way, array.shape[1:], array.dtype) if array.ndim == 2 and way != "stay" else i
        together.setdefault(key, []).append(i)
    results = [None] * len(messages)
    for members in together.values():
        way = messages[members[0]][0]
        if way == "stay":
            results[members[0]] = messages[members[0]][1]
        elif len(members) == 1:
            results[members[0]] = move(way, messages[members[0]][1])
        else:
            whole = move(way, jnp.concatenate([messages[i][1] for i in members], axis=0))
            at = 0
            for i in members:
                rows = messages[i][1].shape[0]
                results[i] = whole[at : at + rows]
                at += rows
    return results


def gather8(block):
    rows = block.shape[0]
    half = rows // 2
    arrays = [block]
    above, below = block, block
    for _ in range(3):
        above, below = yield [up(above), down(below)]
        arrays += [above, below]
    above, below = yield [up(above[:half]), down(below[half:])]
    arrays += [above, below]
    pieces = [(0, 0, rows, 0, 0), (7, 0, half, 4, 0), (8, 0, half, 4, half)]
    for step in (1, 2, 3):
        pieces += [(2 * step - 1, 0, rows, step, 0), (2 * step, 0, rows, 8 - step, 0)]
    return arrays, pieces


def gather16(a, b):
    rows = a.shape[0]
    half = rows // 2
    join = functools.partial(jnp.concatenate, axis=0)
    up1, down1, other_a = yield [up(b), down(b), cross(a)]
    up2, down2, side2 = yield [up(join([a, other_a, up1])), down(join([other_a, a, down1])), cross(join([b, up1, down1]))]
    up3, down3, side3 = yield [up(up2), down(down2), cross(join([up2[2 * rows :], down2[2 * rows :]]))]
    up4, down4, side4 = yield [
        up(up3[: 2 * rows + half]),
        down(join([down3[: 2 * rows], down3[2 * rows + half :]])),
        cross(join([up3[2 * rows :], down3[2 * rows :]])),
    ]
    up5, down5, side5 = yield [up(up4[:rows]), down(down4[:rows]), cross(join([up4[2 * rows :], down4[2 * rows :]]))]
    arrays = [a, b, other_a, up1, down1, up2, down2, side2, up3, down3, side3, up4, down4, side4, up5, down5, side5]
    return arrays, pieces_of(rows)


def pieces_of(rows):
    half = rows // 2
    pieces = [
        (0, 0, rows, 0, 0, 0),
        (1, 0, rows, 1, 0, 0),
        (2, 0, rows, 0, 8, 0),
        (3, 0, rows, 1, 1, 0),
        (4, 0, rows, 1, 7, 0),
        (7, 0, rows, 1, 8, 0),
        (7, rows, rows, 1, 9, 0),
        (7, 2 * rows, rows, 1, 15, 0),
        (10, 0, rows, 1, 10, 0),
        (10, rows, rows, 1, 14, 0),
        (13, 0, rows, 1, 11, 0),
        (13, rows, rows, 1, 13, 0),
        (14, 0, rows, 0, 4, 0),
        (15, 0, rows, 0, 12, 0),
        (16, 0, rows, 1, 12, 0),
        (11, 2 * rows, half, 1, 4, 0),
        (12, 2 * rows, half, 1, 4, half),
        (5, 2 * rows, rows, 1, 2, 0),
        (6, 2 * rows, rows, 1, 6, 0),
        (8, 2 * rows, rows, 1, 3, 0),
        (9, 2 * rows, rows, 1, 5, 0),
    ]
    for step, array in ((1, 5), (2, 8), (3, 11)):
        pieces += [(array, 0, rows, 0, step, 0), (array, rows, rows, 0, 8 + step, 0)]
    for step, array in ((1, 6), (2, 9), (3, 12)):
        pieces += [(array, 0, rows, 0, 16 - step, 0), (array, rows, rows, 0, 8 - step, 0)]
    return pieces


def rounds(*parts):
    results, left, live, back, now = [None] * len(parts), len(parts), {}, {}, 0
    while left:
        for i, (first, part) in enumerate(parts):
            if first == now:
                live[i] = part
        batch = {}
        for i in list(live):
            try:
                batch[i] = live[i].send(back.get(i))
            except StopIteration as end:
                results[i] = end.value
                left -= 1
                del live[i]
        flat = lax.optimization_barrier(sent([message for group in batch.values() for message in group]))
        for i, group in batch.items():
            back[i], flat = flat[: len(group)], flat[len(group) :]
        now += 1
    return results


ROW_TILE = 384


def project_kernel(pieces, first_col, place_ref, half_ref, db_hbm, *refs):
    count = 9
    w_refs = refs[:count]
    keep_k, keep_v, send_k, send_v, db_ref, w_ref, db_sem, w_sem = refs[count:]
    width = w_ref.shape[3]
    db_copy = pltpu.make_async_copy(db_hbm, db_ref, db_sem)
    db_copy.start()
    copies = []
    for i, (array, first, rows, place, at) in enumerate(pieces):
        block = w_ref.shape[2]
        for kind in range(2):
            low, high = max(at, kind * block), min(at + rows, (kind + 1) * block)
            if low < high:
                copies.append(
                    pltpu.make_async_copy(
                        w_refs[array].at[pl.ds(first + low - at, high - low), pl.ds(first_col, width)],
                        w_ref.at[kind, place_ref[place], pl.ds(low - kind * block, high - low)],
                        w_sem.at[len(copies)],
                    )
                )
                copies[-1].start()
    db_copy.wait()
    for copy in copies:
        copy.wait()
    depth = w_ref.shape[1] * w_ref.shape[2]
    six = 2 * HELD
    turns = db_ref.shape[0] // 2 // (2 * six * 16)
    per_tile = ROW_TILE // (2 * six * 16)
    for own in (0, 1):
        side = half_ref[0] if own else 1 - half_ref[0]
        for tile in range(turns // per_tile):
            start = pl.multiple_of(side * (turns * 2 * six * 16) + tile * ROW_TILE, ROW_TILE)
            rows = db_ref[pl.ds(start, ROW_TILE), :]
            for kind in (0, 1):
                part = jnp.dot(rows, w_ref[kind].reshape(depth, width), preferred_element_type=F32)
                for j in range(ROW_TILE // 16):
                    turn, entry = divmod(j, 2 * six)
                    other, entry = divmod(entry, six)
                    at = entry * TOK + (tile * per_tile + turn) * 16
                    piece = part[j * 16 : (j + 1) * 16]
                    if kind == 0 and other:
                        at += (1 - own) * six * TOK
                        send_k[at : at + 16, :] = piece.astype(BF)
                    elif kind == 0:
                        keep_k[1 - own, at : at + 16, :] = piece
                    elif own:
                        keep_v[other, at : at + 16, :] = piece
                    else:
                        at += other * six * TOK
                        send_v[at : at + 16, :] = piece.astype(BF)


def project(db, arrays, pieces, places, side, first_col, width):
    rows, depth = db.shape
    block = rows // 4
    vmem = pl.BlockSpec(memory_space=pltpu.VMEM)
    anywhere = pl.BlockSpec(memory_space=pl.ANY)
    smem = pl.BlockSpec(memory_space=pltpu.SMEM)
    return pl.pallas_call(
        functools.partial(project_kernel, pieces, first_col),
        out_shape=[jax.ShapeDtypeStruct((2, block, width), F32)] * 2 + [jax.ShapeDtypeStruct((2 * block, width), BF)] * 2,
        in_specs=[smem, smem] + [anywhere] * (1 + len(arrays)),
        out_specs=[vmem] * 4,
        scratch_shapes=[
            pltpu.VMEM((rows, depth), BF),
            pltpu.VMEM((2, ZN, depth // ZN, width), BF),
            pltpu.SemaphoreType.DMA,
            pltpu.SemaphoreType.DMA((2 * len(pieces),)),
        ],
        compiler_params=pltpu.CompilerParams(vmem_limit_bytes=60 << 20),
        cost_estimate=pl.CostEstimate(flops=4 * rows * depth * width, bytes_accessed=12 << 20, transcendentals=0),
        name="project",
    )(places, side, db, *arrays)


TASKS = 16


def attend_kernel(pieces, first_col, parts, slot_ref, *refs):
    count = 17
    q_parts = refs[:parts]
    kv_refs = refs[parts : parts + count]
    out_ref, stat_ref, q_ref, kv_ref, q_sem, sem = refs[parts + count :]
    width = kv_ref.shape[2]
    copies = []
    begin = 0
    for i, source in enumerate(q_parts):
        rows = source.shape[0]
        copies.append(
            pltpu.make_async_copy(source.at[:, pl.ds(first_col, width)], q_ref.at[pl.ds(begin, rows)], q_sem.at[i])
        )
        copies[-1].start()
        begin += rows
    for i, (array, first, rows, kind, place, at) in enumerate(pieces):
        copies.append(
            pltpu.make_async_copy(
                kv_refs[array].at[pl.ds(first, rows)],
                kv_ref.at[kind, pl.ds(place * 6 * TOK + at, rows)],
                sem.at[i],
            )
        )
        copies[-1].start()
    for copy in copies:
        copy.wait()
    lane = lax.broadcasted_iota(jnp.int32, (SEGMENT, 128), 1)
    heads = width // HDIM
    at_once = TASKS // max(heads, 1) if heads != 3 else 4

    def group(g, stat):
        tasks, scores, results = [], [], []
        for i in range(at_once):
            u = g * at_once + i
            at = pl.multiple_of(u * SEGMENT, SEGMENT)
            one = pl.multiple_of(slot_ref[2 * u] * TOK, TOK)
            two = pl.multiple_of(slot_ref[2 * u + 1] * TOK, TOK)
            for j in range(heads):
                tasks.append((u, at, one, two, j, slice(j * HDIM, (j + 1) * HDIM)))
        for u, at, one, two, j, cols in tasks:
            q = q_ref[pl.ds(at, SEGMENT), cols]
            keys = jnp.concatenate([kv_ref[0, pl.ds(one, TOK), cols], kv_ref[0, pl.ds(two, TOK), cols]], axis=0)
            score = lax.dot_general(q, keys, (((1,), (1,)), ((), ())), preferred_element_type=F32)
            scores.append(score * (HDIM**-0.5))
        tops = [jnp.max(score, axis=1, keepdims=True) for score in scores]
        weights = [jnp.exp(score - top) for score, top in zip(scores, tops)]
        for (u, at, one, two, j, cols), weight in zip(tasks, weights):
            values = jnp.concatenate([kv_ref[1, pl.ds(one, TOK), cols], kv_ref[1, pl.ds(two, TOK), cols]], axis=0)
            mixed = jnp.dot(weight.astype(BF), values, preferred_element_type=F32)
            results.append((mixed, jnp.sum(weight, axis=1, keepdims=True)))
        for (u, at, one, two, j, cols), (mixed, total), top in zip(tasks, results, tops):
            out_ref[pl.ds(at, SEGMENT), cols] = (mixed / total).astype(BF)
            stat = jnp.where(lane == u * heads + j, top + jnp.log(total), stat)
        return stat

    segments = q_ref.shape[0] // SEGMENT
    stat_ref[...] = lax.fori_loop(0, segments // at_once, group, jnp.zeros((SEGMENT, 128), F32))


def attend(slots, query_parts, first_col, arrays, pieces):
    rows = sum(part.shape[0] for part in query_parts)
    block, width = arrays[0].shape
    smem = pl.BlockSpec(memory_space=pltpu.SMEM)
    vmem = pl.BlockSpec(memory_space=pltpu.VMEM)
    anywhere = pl.BlockSpec(memory_space=pl.ANY)
    return pl.pallas_call(
        functools.partial(attend_kernel, pieces, first_col, len(query_parts)),
        out_shape=[jax.ShapeDtypeStruct((rows, width), BF), jax.ShapeDtypeStruct((SEGMENT, 128), F32)],
        in_specs=[smem] + [anywhere] * (len(query_parts) + len(arrays)),
        out_specs=[vmem] * 2,
        scratch_shapes=[
            pltpu.VMEM((rows, width), BF),
            pltpu.VMEM((2, 16 * block, width), BF),
            pltpu.SemaphoreType.DMA((len(query_parts),)),
            pltpu.SemaphoreType.DMA((len(pieces),)),
        ],
        compiler_params=pltpu.CompilerParams(vmem_limit_bytes=60 << 20),
        cost_estimate=pl.CostEstimate(flops=4 * rows * 128 * width, bytes_accessed=10 << 20, transcendentals=rows * width),
        name="attend",
    )(slots, *query_parts, *arrays)


def merge_kernel(first_col, mine_ref, theirs_ref, stat_ref, other_ref, *refs):
    out_hbm, out_ref, sem = refs[-3:]
    lane = lax.broadcasted_iota(jnp.int32, (SEGMENT, 128), 1)
    width = mine_ref.shape[1]
    heads = width // HDIM
    difference = other_ref[...] - stat_ref[...]

    def unit(u, carry):
        at = pl.multiple_of(u * SEGMENT, SEGMENT)
        for j in range(heads):
            cols = slice(j * HDIM, (j + 1) * HDIM)
            gap = jnp.sum(jnp.where(lane == u * heads + j, difference, 0.0), axis=1, keepdims=True)
            small = jnp.exp(-jnp.abs(gap))
            larger = 1.0 / (1.0 + small)
            smaller = small * larger
            share = jnp.where(gap > 0, smaller, larger)
            rest = jnp.where(gap > 0, larger, smaller)
            a = mine_ref[pl.ds(at, SEGMENT), cols].astype(F32)
            b = theirs_ref[pl.ds(at, SEGMENT), cols].astype(F32)
            out_ref[pl.ds(at, SEGMENT), cols] = (a * share + b * rest).astype(BF)
        return carry

    lax.fori_loop(0, mine_ref.shape[0] // SEGMENT, unit, 0, unroll=8)
    copy = pltpu.make_async_copy(out_ref, out_hbm.at[:, pl.ds(first_col, width)], sem)
    copy.start()
    copy.wait()


def merge(mine, theirs, stat, other, first_col, columns, so_far):
    rows, width = mine.shape
    vmem = pl.BlockSpec(memory_space=pltpu.VMEM)
    anywhere = pl.BlockSpec(memory_space=pl.ANY)
    extra = [] if so_far is None else [so_far]
    return pl.pallas_call(
        functools.partial(merge_kernel, first_col),
        out_shape=jax.ShapeDtypeStruct((rows, columns), BF),
        in_specs=[vmem] * 4 + [anywhere] * len(extra),
        out_specs=anywhere,
        scratch_shapes=[pltpu.VMEM((rows, width), BF), pltpu.SemaphoreType.DMA],
        input_output_aliases={4: 0} if extra else {},
        compiler_params=pltpu.CompilerParams(vmem_limit_bytes=24 << 20),
        cost_estimate=pl.CostEstimate(flops=8 * rows * width, bytes_accessed=6 * rows * width, transcendentals=rows),
        name="merge",
    )(mine, theirs, stat, other, *extra)


def local(db_states, w_key, w_value, queries, nbr_owner, nbr_row):
    place = lax.axis_index("dp")
    x, z = place // ZN, place % ZN
    side = ((x + 1) // 2) % 2
    quarter = db_states.shape[2] // XN
    rows, columns = queries.shape

    def quarter_of(which):
        return lax.dynamic_slice_in_dim(db_states, which * quarter, quarter, axis=2)

    def database():
        by_pair, by_cross, by_diagonal = yield [
            pair(quarter_of(x ^ 1)),
            cross(quarter_of(x ^ 3)),
            diagonal(quarter_of(x ^ 2)),
        ]
        own, even = quarter_of(x), x % 2 == 0
        order = [
            jnp.where(even, own, by_pair),
            jnp.where(even, by_pair, own),
            jnp.where(even, by_diagonal, by_cross),
            jnp.where(even, by_cross, by_diagonal),
        ]
        twelve = jnp.concatenate(order, axis=0)
        return lax.all_gather(twelve, "mp", axis=0, tiled=False).reshape(-1, quarter)

    def query_part(i):
        return pair(queries[i * rows // 4 : (i + 1) * rows // 4])

    def early_queries():
        parts = yield [query_part(0)]
        parts += yield [query_part(1)]
        last, tables = yield [query_part(2), pair(jnp.concatenate([nbr_owner, nbr_row], axis=1))]
        return [*parts, last], tables

    (w_arrays, w_pieces), db, (their_parts, tables) = rounds(
        (0, gather8(jnp.concatenate([w_key, w_value], axis=0))), (0, database()), (1, early_queries())
    )

    places = ((z - jnp.arange(ZN)) % ZN).astype(jnp.int32)
    flag = side.reshape(1).astype(jnp.int32)

    def slots(owner, row):
        from_x, from_z = owner // ZN, owner % ZN
        block = jnp.where(from_x // 2 == x // 2, 0, ZN) + (z - from_z) % ZN
        return (block * (2 * HELD) + (from_x % 2) * HELD + row).reshape(-1).astype(jnp.int32)

    own_slots = slots(nbr_owner, nbr_row)
    their_slots = slots(tables[:, :2], tables[:, 2:])

    shares = [project(db, w_arrays, w_pieces, places, flag, first * HDIM, heads * HDIM) for first, heads in CHUNKS]

    def summed(share):
        keep_k, keep_v, send_k, send_v = share
        got_k, got_v = yield [cross(send_k), pair(send_v)]
        half = send_k.shape[0] // 2
        pass_k = (keep_k[1] + got_k[half:].astype(F32)).astype(BF)
        pass_v = (keep_v[1] + got_v[half:].astype(F32)).astype(BF)
        last_k, last_v = yield [pair(pass_k), cross(pass_v)]
        keys = (keep_k[0] + got_k[:half].astype(F32) + last_k.astype(F32)).astype(BF)
        values = (keep_v[0] + got_v[:half].astype(F32) + last_v.astype(F32)).astype(BF)
        return keys, values

    found = {}

    def first_chunk():
        keys, values = yield from summed(shares[0])
        found[0] = yield from gather16(keys, values)

    def second_chunk():
        yield [stay(array) for array in shares[1]]
        for _ in range(3):
            yield []
        keys, values = yield from summed(shares[1])
        found[1] = yield from gather16(keys, values)

    def last_queries():
        their_parts.extend((yield [query_part(3)]))

    results = []

    def answers():
        given, stat = attend(their_slots, their_parts, CHUNKS[0][0] * HDIM, *found[0])
        yield []
        mine, own_stat = attend(own_slots, [queries], CHUNKS[0][0] * HDIM, *found[0])
        theirs, other, mine, own_stat = yield [pair(given), pair(stat), stay(mine), stay(own_stat)]
        results.append((mine, theirs, own_stat, other))

    rounds((0, first_chunk()), (0, second_chunk()), (6, last_queries()), (7, answers()))
    first_col = CHUNKS[1][0] * HDIM
    given, stat = attend(their_slots, their_parts, first_col, *found[1])
    theirs, other = move("pair", given), move("pair", stat)
    output = merge(*results[0], CHUNKS[0][0] * HDIM, columns, None)
    mine, own_stat = attend(own_slots, [queries], first_col, *found[1])
    return merge(mine, theirs, own_stat, other, first_col, columns, output)


def solution(mesh):
    in_specs = (
        P("dp", "mp", None),
        P("dp", "mp"),
        P("dp", "mp"),
        P("dp", "mp"),
        P("dp", None),
        P("dp", None),
    )
    out_specs = P("dp", "mp")
    return jax.shard_map(local, mesh=mesh, in_specs=in_specs, out_specs=out_specs, check_vma=False)
```

```python
import functools

import jax
import jax.numpy as jnp
from jax import lax
from jax.experimental import pallas as pl
from jax.experimental.pallas import tpu as pltpu
from jax.sharding import PartitionSpec as P

HDIM = 128
SEGMENT = 64
XN, ZN = 4, 8
HELD = 3
TOK = 64
CHUNKS = ((0, 2), (2, 2))
BF = jnp.bfloat16
F32 = jnp.float32


WAYS = {
    "up": lambda x, z: (x, z + 1),
    "down": lambda x, z: (x, z - 1),
    "cross": lambda x, z: (x ^ 3, z),
    "pair": lambda x, z: (x ^ 1, z),
    "diagonal": lambda x, z: (x ^ 2, z),
}


def move(way, array):
    pairs = []
    for x in range(XN):
        for z in range(ZN):
            tx, tz = WAYS[way](x, z)
            pairs.append((x * ZN + z, tx * ZN + tz % ZN))
    return lax.ppermute(array, "dp", pairs)


def up(array):
    return "up", array


def down(array):
    return "down", array


def cross(array):
    return "cross", array


def pair(array):
    return "pair", array


def diagonal(array):
    return "diagonal", array


def stay(array):
    return "stay", array


def sent(messages):
    together = {}
    for i, (way, array) in enumerate(messages):
        key = (way, array.shape[1:], array.dtype) if array.ndim == 2 and way != "stay" else i
        together.setdefault(key, []).append(i)
    results = [None] * len(messages)
    for members in together.values():
        way = messages[members[0]][0]
        if way == "stay":
            results[members[0]] = messages[members[0]][1]
        elif len(members) == 1:
            results[members[0]] = move(way, messages[members[0]][1])
        else:
            whole = move(way, jnp.concatenate([messages[i][1] for i in members], axis=0))
            at = 0
            for i in members:
                rows = messages[i][1].shape[0]
                results[i] = whole[at : at + rows]
                at += rows
    return results


def gather8(block):
    rows = block.shape[0]
    half = rows // 2
    arrays = [block]
    above, below = block, block
    for _ in range(3):
        above, below = yield [up(above), down(below)]
        arrays += [above, below]
    above, below = yield [up(above[:half]), down(below[half:])]
    arrays += [above, below]
    pieces = [(0, 0, rows, 0, 0), (7, 0, half, 4, 0), (8, 0, half, 4, half)]
    for step in (1, 2, 3):
        pieces += [(2 * step - 1, 0, rows, step, 0), (2 * step, 0, rows, 8 - step, 0)]
    return arrays, pieces


def gather16(a, b):
    rows = a.shape[0]
    half = rows // 2
    join = functools.partial(jnp.concatenate, axis=0)
    up1, down1, other_a = yield [up(b), down(b), cross(a)]
    up2, down2, side2 = yield [up(join([a, other_a, up1])), down(join([other_a, a, down1])), cross(join([b, up1, down1]))]
    up3, down3, side3 = yield [up(up2), down(down2), cross(join([up2[2 * rows :], down2[2 * rows :]]))]
    up4, down4, side4 = yield [
        up(up3[: 2 * rows + half]),
        down(join([down3[: 2 * rows], down3[2 * rows + half :]])),
        cross(join([up3[2 * rows :], down3[2 * rows :]])),
    ]
    up5, down5, side5 = yield [up(up4[:rows]), down(down4[:rows]), cross(join([up4[2 * rows :], down4[2 * rows :]]))]
    arrays = [a, b, other_a, up1, down1, up2, down2, side2, up3, down3, side3, up4, down4, side4, up5, down5, side5]
    return arrays, pieces_of(rows)


def pieces_of(rows):
    half = rows // 2
    pieces = [
        (0, 0, rows, 0, 0, 0),
        (1, 0, rows, 1, 0, 0),
        (2, 0, rows, 0, 8, 0),
        (3, 0, rows, 1, 1, 0),
        (4, 0, rows, 1, 7, 0),
        (7, 0, rows, 1, 8, 0),
        (7, rows, rows, 1, 9, 0),
        (7, 2 * rows, rows, 1, 15, 0),
        (10, 0, rows, 1, 10, 0),
        (10, rows, rows, 1, 14, 0),
        (13, 0, rows, 1, 11, 0),
        (13, rows, rows, 1, 13, 0),
        (14, 0, rows, 0, 4, 0),
        (15, 0, rows, 0, 12, 0),
        (16, 0, rows, 1, 12, 0),
        (11, 2 * rows, half, 1, 4, 0),
        (12, 2 * rows, half, 1, 4, half),
        (5, 2 * rows, rows, 1, 2, 0),
        (6, 2 * rows, rows, 1, 6, 0),
        (8, 2 * rows, rows, 1, 3, 0),
        (9, 2 * rows, rows, 1, 5, 0),
    ]
    for step, array in ((1, 5), (2, 8), (3, 11)):
        pieces += [(array, 0, rows, 0, step, 0), (array, rows, rows, 0, 8 + step, 0)]
    for step, array in ((1, 6), (2, 9), (3, 12)):
        pieces += [(array, 0, rows, 0, 16 - step, 0), (array, rows, rows, 0, 8 - step, 0)]
    return pieces


def rounds(*parts):
    results, left, live, back, now = [None] * len(parts), len(parts), {}, {}, 0
    while left:
        for i, (first, part) in enumerate(parts):
            if first == now:
                live[i] = part
        batch = {}
        for i in list(live):
            try:
                batch[i] = live[i].send(back.get(i))
            except StopIteration as end:
                results[i] = end.value
                left -= 1
                del live[i]
        flat = lax.optimization_barrier(sent([message for group in batch.values() for message in group]))
        for i, group in batch.items():
            back[i], flat = flat[: len(group)], flat[len(group) :]
        now += 1
    return results


ROW_TILE = 768


def project_kernel(pieces, first_col, split, place_ref, half_ref, db_hbm, *refs):
    count = 9
    w_refs = refs[:count]
    keep_k, keep_v, send_k, send_v, db_ref, w_ref, db_sem, w_sem = refs[count:]
    width = w_ref.shape[2] // 2
    copies = []
    for array, first, rows, place, at in pieces:
        block = w_ref.shape[1]
        for kind in range(2):
            low, high = max(at, kind * block), min(at + rows, (kind + 1) * block)
            if low < high:
                copies.append(
                    pltpu.make_async_copy(
                        w_refs[array].at[pl.ds(first + low - at, high - low), pl.ds(first_col, width)],
                        w_ref.at[place_ref[place], pl.ds(low - kind * block, high - low), pl.ds(kind * width, width)],
                        w_sem.at[len(copies)],
                    )
                )
                copies[-1].start()
    depth = w_ref.shape[0] * w_ref.shape[1]
    six = 2 * HELD
    turns = db_ref.shape[0] // 2 // (2 * six * 16)
    per_tile = ROW_TILE // (2 * six * 16)
    tiles = [(own, tile) for own in (0, 1) for tile in range(turns // per_tile)]
    loads = []
    for i, (own, tile) in enumerate(tiles):
        side = half_ref[0] if own else 1 - half_ref[0]
        start = pl.multiple_of(side * (turns * 2 * six * 16) + tile * ROW_TILE, ROW_TILE)
        loads.append(
            pltpu.make_async_copy(
                db_hbm.at[pl.ds(start, ROW_TILE)], db_ref.at[pl.ds(i * ROW_TILE, ROW_TILE)], db_sem.at[i]
            )
        )
        loads[-1].start()
    for copy in copies:
        copy.wait()
    for i, (own, tile) in enumerate(tiles):
        loads[i].wait()
        rows = db_ref[i * ROW_TILE : (i + 1) * ROW_TILE, :]
        part = jnp.dot(rows, w_ref[...].reshape(depth, 2 * width), preferred_element_type=F32)
        for j in range(ROW_TILE // 16):
            turn, entry = divmod(j, 2 * six)
            other, entry = divmod(entry, six)
            token = entry * TOK + (tile * per_tile + turn) * 16
            for kind, keep, send in ((0, keep_k, send_k), (1, keep_v, send_v)):
                at = token
                piece = part[j * 16 : (j + 1) * 16, kind * width : (kind + 1) * width]
                if split and kind == 0 and other:
                    at += (1 - own) * six * TOK
                    send[at : at + 16, :] = piece.astype(BF)
                elif split and kind == 0:
                    keep[1 - own, at : at + 16, :] = piece
                elif own:
                    keep[other, at : at + 16, :] = piece
                else:
                    at += other * six * TOK
                    send[at : at + 16, :] = piece.astype(BF)


def project(db, arrays, pieces, places, side, first_col, width, split):
    rows, depth = db.shape
    block = rows // 4
    vmem = pl.BlockSpec(memory_space=pltpu.VMEM)
    anywhere = pl.BlockSpec(memory_space=pl.ANY)
    smem = pl.BlockSpec(memory_space=pltpu.SMEM)
    return pl.pallas_call(
        functools.partial(project_kernel, pieces, first_col, split),
        out_shape=[jax.ShapeDtypeStruct((2, block, width), F32)] * 2 + [jax.ShapeDtypeStruct((2 * block, width), BF)] * 2,
        in_specs=[smem, smem] + [anywhere] * (1 + len(arrays)),
        out_specs=[vmem] * 4,
        scratch_shapes=[
            pltpu.VMEM((rows, depth), BF),
            pltpu.VMEM((ZN, depth // ZN, 2 * width), BF),
            pltpu.SemaphoreType.DMA((rows // ROW_TILE,)),
            pltpu.SemaphoreType.DMA((2 * len(pieces),)),
        ],
        compiler_params=pltpu.CompilerParams(vmem_limit_bytes=60 << 20),
        cost_estimate=pl.CostEstimate(flops=4 * rows * depth * width, bytes_accessed=12 << 20, transcendentals=0),
        name="project",
    )(places, side, db, *arrays)


TASKS = 16


def attend_kernel(pieces, first_col, layout, slot_ref, *refs):
    count = 17
    parts = sum(len(given) for given, _ in layout)
    outs = sum(len(made) for _, made in layout)
    q_refs, kv_refs, refs = refs[:parts], refs[parts : parts + count], refs[parts + count :]
    out_refs, stat_refs = refs[:outs], refs[outs : outs + len(layout)]
    q_ref, kv_ref, q_sem, sem = refs[outs + len(layout) :]
    width = kv_ref.shape[2]
    copies = []
    begin = 0
    for i, source in enumerate(q_refs):
        rows = source.shape[0]
        copies.append(
            pltpu.make_async_copy(source.at[:, pl.ds(first_col, width)], q_ref.at[pl.ds(begin, rows)], q_sem.at[i])
        )
        copies[-1].start()
        begin += rows
    for i, (array, first, rows, kind, place, at) in enumerate(pieces):
        copies.append(
            pltpu.make_async_copy(
                kv_refs[array].at[pl.ds(first, rows)],
                kv_ref.at[kind, pl.ds(place * 6 * TOK + at, rows)],
                sem.at[i],
            )
        )
        copies[-1].start()
    for copy in copies:
        copy.wait()
    lane = lax.broadcasted_iota(jnp.int32, (SEGMENT, 128), 1)
    heads = width // HDIM
    at_once = TASKS // heads

    def group(g, stat, segment, first, out_ref):
        tasks, scores, results = [], [], []
        for i in range(at_once):
            u = g * at_once + i
            at = pl.multiple_of(u * SEGMENT, SEGMENT)
            one = pl.multiple_of(slot_ref[2 * (segment + u)] * TOK, TOK)
            two = pl.multiple_of(slot_ref[2 * (segment + u) + 1] * TOK, TOK)
            for j in range(heads):
                tasks.append((first + u, at, one, two, j, slice(j * HDIM, (j + 1) * HDIM)))
        for u, at, one, two, j, cols in tasks:
            q = q_ref[pl.ds(segment * SEGMENT + at, SEGMENT), cols]
            keys = jnp.concatenate([kv_ref[0, pl.ds(one, TOK), cols], kv_ref[0, pl.ds(two, TOK), cols]], axis=0)
            score = lax.dot_general(q, keys, (((1,), (1,)), ((), ())), preferred_element_type=F32)
            scores.append(score * (HDIM**-0.5))
        tops = [jnp.max(score, axis=1, keepdims=True) for score in scores]
        weights = [jnp.exp(score - top) for score, top in zip(scores, tops)]
        for (u, at, one, two, j, cols), weight in zip(tasks, weights):
            values = jnp.concatenate([kv_ref[1, pl.ds(one, TOK), cols], kv_ref[1, pl.ds(two, TOK), cols]], axis=0)
            mixed = jnp.dot(weight.astype(BF), values, preferred_element_type=F32)
            results.append((mixed, jnp.sum(weight, axis=1, keepdims=True)))
        for (u, at, one, two, j, cols), (mixed, total), top in zip(tasks, results, tops):
            out_ref[pl.ds(at, SEGMENT), cols] = (mixed / total).astype(BF)
            stat = jnp.where(lane == u * heads + j, top + jnp.log(total), stat)
        return stat

    segment = 0
    out_refs = list(out_refs)
    for (_, made), stat_ref in zip(layout, stat_refs):
        first, stat = 0, jnp.zeros((SEGMENT, 128), F32)
        for rows in made:
            step = functools.partial(group, segment=segment, first=first, out_ref=out_refs.pop(0))
            stat = lax.fori_loop(0, rows // SEGMENT // at_once, step, stat)
            segment += rows // SEGMENT
            first += rows // SEGMENT
        stat_ref[...] = stat


def attend(sides, first_col, arrays, pieces):
    layout = [([part.shape[0] for part in parts], made) for _, parts, made in sides]
    queries = [part for _, parts, _ in sides for part in parts]
    slots = jnp.concatenate([slots for slots, _, _ in sides])
    outs = [rows for _, _, made in sides for rows in made]
    total = sum(outs)
    block, width = arrays[0].shape
    smem = pl.BlockSpec(memory_space=pltpu.SMEM)
    vmem = pl.BlockSpec(memory_space=pltpu.VMEM)
    anywhere = pl.BlockSpec(memory_space=pl.ANY)
    return pl.pallas_call(
        functools.partial(attend_kernel, pieces, first_col, layout),
        out_shape=[jax.ShapeDtypeStruct((rows, width), BF) for rows in outs]
        + [jax.ShapeDtypeStruct((SEGMENT, 128), F32)] * len(sides),
        in_specs=[smem] + [anywhere] * (len(queries) + len(arrays)),
        out_specs=[vmem] * (len(outs) + len(sides)),
        scratch_shapes=[
            pltpu.VMEM((total, width), BF),
            pltpu.VMEM((2, 16 * block, width), BF),
            pltpu.SemaphoreType.DMA((len(queries),)),
            pltpu.SemaphoreType.DMA((len(pieces),)),
        ],
        compiler_params=pltpu.CompilerParams(vmem_limit_bytes=60 << 20),
        cost_estimate=pl.CostEstimate(flops=4 * total * 128 * width, bytes_accessed=10 << 20, transcendentals=total * width),
        name="attend",
    )(slots, *queries, *arrays)


def merge_kernel(first_col, parts, mine_ref, stat_ref, other_ref, *refs):
    out_hbm, out_ref, sem = refs[-3:]
    lane = lax.broadcasted_iota(jnp.int32, (SEGMENT, 128), 1)
    width = mine_ref.shape[1]
    heads = width // HDIM
    difference = other_ref[...] - stat_ref[...]

    def unit(u, carry, first, theirs_ref):
        at = pl.multiple_of((first + u) * SEGMENT, SEGMENT)
        there = pl.multiple_of(u * SEGMENT, SEGMENT)
        for j in range(heads):
            cols = slice(j * HDIM, (j + 1) * HDIM)
            gap = jnp.sum(jnp.where(lane == (first + u) * heads + j, difference, 0.0), axis=1, keepdims=True)
            small = jnp.exp(-jnp.abs(gap))
            larger = 1.0 / (1.0 + small)
            smaller = small * larger
            share = jnp.where(gap > 0, smaller, larger)
            rest = jnp.where(gap > 0, larger, smaller)
            a = mine_ref[pl.ds(at, SEGMENT), cols].astype(F32)
            b = theirs_ref[pl.ds(there, SEGMENT), cols].astype(F32)
            out_ref[pl.ds(at, SEGMENT), cols] = (a * share + b * rest).astype(BF)
        return carry

    first = 0
    for theirs_ref in refs[:parts]:
        segments = theirs_ref.shape[0] // SEGMENT
        lax.fori_loop(0, segments, functools.partial(unit, first=first, theirs_ref=theirs_ref), 0, unroll=8)
        first += segments
    copy = pltpu.make_async_copy(out_ref, out_hbm.at[:, pl.ds(first_col, width)], sem)
    copy.start()
    copy.wait()


def merge(mine, theirs, stat, other, first_col, columns, so_far):
    rows, width = mine.shape
    vmem = pl.BlockSpec(memory_space=pltpu.VMEM)
    anywhere = pl.BlockSpec(memory_space=pl.ANY)
    extra = [] if so_far is None else [so_far]
    return pl.pallas_call(
        functools.partial(merge_kernel, first_col, len(theirs)),
        out_shape=jax.ShapeDtypeStruct((rows, columns), BF),
        in_specs=[vmem] * (3 + len(theirs)) + [anywhere] * len(extra),
        out_specs=anywhere,
        scratch_shapes=[pltpu.VMEM((rows, width), BF), pltpu.SemaphoreType.DMA],
        input_output_aliases={3 + len(theirs): 0} if extra else {},
        compiler_params=pltpu.CompilerParams(vmem_limit_bytes=24 << 20),
        cost_estimate=pl.CostEstimate(flops=8 * rows * width, bytes_accessed=6 * rows * width, transcendentals=rows),
        name="merge",
    )(mine, stat, other, *theirs, *extra)


def local(db_states, w_key, w_value, queries, nbr_owner, nbr_row):
    place = lax.axis_index("dp")
    x, z = place // ZN, place % ZN
    side = ((x + 1) // 2) % 2
    quarter = db_states.shape[2] // XN
    rows, columns = queries.shape

    def quarter_of(which):
        return lax.dynamic_slice_in_dim(db_states, which * quarter, quarter, axis=2)

    def database():
        by_pair, by_cross, by_diagonal = yield [
            pair(quarter_of(x ^ 1)),
            cross(quarter_of(x ^ 3)),
            diagonal(quarter_of(x ^ 2)),
        ]
        own, even = quarter_of(x), x % 2 == 0
        order = [
            jnp.where(even, own, by_pair),
            jnp.where(even, by_pair, own),
            jnp.where(even, by_diagonal, by_cross),
            jnp.where(even, by_cross, by_diagonal),
        ]
        twelve = jnp.concatenate(order, axis=0)
        return lax.all_gather(twelve, "mp", axis=0, tiled=False).reshape(-1, quarter)

    def query_part(first, last):
        return pair(queries[first * rows // 16 : last * rows // 16])

    def early_queries():
        parts = yield [query_part(0, 5)]
        parts += yield [query_part(5, 10)]
        last, tables = yield [query_part(10, 13), pair(jnp.concatenate([nbr_owner, nbr_row], axis=1))]
        return [*parts, last], tables

    (w_arrays, w_pieces), db, (their_parts, tables) = rounds(
        (0, gather8(jnp.concatenate([w_key, w_value], axis=0))), (0, database()), (1, early_queries())
    )

    places = ((z - jnp.arange(ZN)) % ZN).astype(jnp.int32)
    flag = side.reshape(1).astype(jnp.int32)

    def slots(owner, row):
        from_x, from_z = owner // ZN, owner % ZN
        block = jnp.where(from_x // 2 == x // 2, 0, ZN) + (z - from_z) % ZN
        return (block * (2 * HELD) + (from_x % 2) * HELD + row).reshape(-1).astype(jnp.int32)

    own_slots = slots(nbr_owner, nbr_row)
    their_slots = slots(tables[:, :2], tables[:, 2:])

    shares = [
        project(db, w_arrays, w_pieces, places, flag, first * HDIM, heads * HDIM, first == 0) for first, heads in CHUNKS
    ]

    def plus(kept, *got):
        return sum([part.astype(F32) for part in got], kept).astype(BF)

    def summed_both_ways(share):
        keep_k, keep_v, send_k, send_v = share
        got_k, got_v = yield [cross(send_k), pair(send_v)]
        half = send_k.shape[0] // 2
        last_k, last_v = yield [pair(plus(keep_k[1], got_k[half:])), cross(plus(keep_v[1], got_v[half:]))]
        return plus(keep_k[0], got_k[:half], last_k), plus(keep_v[0], got_v[:half], last_v)

    def summed_pair_first(share):
        keep_k, keep_v, send_k, send_v = share
        half = send_k.shape[0] // 2
        (got_v,) = yield [pair(send_v)]
        got_k, last_v = yield [pair(send_k), cross(plus(keep_v[1], got_v[half:]))]
        (last_k,) = yield [cross(plus(keep_k[1], got_k[half:]))]
        return plus(keep_k[0], got_k[:half], last_k), plus(keep_v[0], got_v[:half], last_v)

    found = {}

    def first_chunk():
        keys, values = yield from summed_both_ways(shares[0])
        found[0] = yield from gather16(keys, values)

    def second_chunk():
        yield [stay(array) for array in shares[1]]
        yield []
        yield []
        keys, values = yield from summed_pair_first(shares[1])
        found[1] = yield from gather16(keys, values)

    def last_queries():
        their_parts.extend((yield [query_part(13, 16)]))

    results = []

    def answers():
        sides = [(their_slots, their_parts, [rows // 2, rows // 2]), (own_slots, [queries], [rows])]
        upper, lower, mine, stat, own_stat = attend(sides, CHUNKS[0][0] * HDIM, *found[0])
        lower, mine, stat, own_stat = yield [stay(lower), stay(mine), stay(stat), stay(own_stat)]
        upper, other = yield [pair(upper), pair(stat)]
        (lower,) = yield [pair(lower)]
        results.append((mine, [upper, lower], own_stat, other))

    rounds((0, first_chunk()), (0, second_chunk()), (6, last_queries()), (7, answers()))
    first_col = CHUNKS[1][0] * HDIM
    given, stat = attend([(their_slots, their_parts, [rows])], first_col, *found[1])
    theirs, other = move("pair", given), move("pair", stat)
    output = merge(*results[0], CHUNKS[0][0] * HDIM, columns, None)
    mine, own_stat = attend([(own_slots, [queries], [rows])], first_col, *found[1])
    return merge(mine, [theirs], own_stat, other, first_col, columns, output)


def solution(mesh):
    in_specs = (
        P("dp", "mp", None),
        P("dp", "mp"),
        P("dp", "mp"),
        P("dp", "mp"),
        P("dp", None),
        P("dp", None),
    )
    out_specs = P("dp", "mp")
    return jax.shard_map(local, mesh=mesh, in_specs=in_specs, out_specs=out_specs, check_vma=False)
```

```python
import functools

import jax
import jax.numpy as jnp
from jax import lax
from jax.experimental import pallas as pl
from jax.experimental.pallas import tpu as pltpu
from jax.sharding import PartitionSpec as P

HDIM = 128
SEGMENT = 64
XN, ZN = 4, 8
HELD = 3
TOK = 64
CHUNKS = ((0, 2), (2, 2))
BF = jnp.bfloat16
F32 = jnp.float32


WAYS = {
    "up": lambda x, z: (x, z + 1),
    "down": lambda x, z: (x, z - 1),
    "cross": lambda x, z: (x ^ 3, z),
    "pair": lambda x, z: (x ^ 1, z),
    "diagonal": lambda x, z: (x ^ 2, z),
}


def move(way, array):
    pairs = []
    for x in range(XN):
        for z in range(ZN):
            tx, tz = WAYS[way](x, z)
            pairs.append((x * ZN + z, tx * ZN + tz % ZN))
    return lax.ppermute(array, "dp", pairs)


def up(array):
    return "up", array


def down(array):
    return "down", array


def cross(array):
    return "cross", array


def pair(array):
    return "pair", array


def diagonal(array):
    return "diagonal", array


def stay(array):
    return "stay", array


class Part:
    def __init__(self, whole, first, rows):
        self.whole, self.first, self.rows = whole, first, rows

    @property
    def array(self):
        if self.rows == self.whole.shape[0]:
            return self.whole
        return self.whole[self.first : self.first + self.rows]


def sent(messages):
    together = {}
    for i, (way, array) in enumerate(messages):
        key = (way, array.shape[1:], array.dtype) if array.ndim == 2 and way != "stay" else i
        together.setdefault(key, []).append(i)
    wholes, spots = [], [None] * len(messages)
    for members in together.values():
        way = messages[members[0]][0]
        joined = [messages[i][1] for i in members]
        whole = joined[0] if len(joined) == 1 else jnp.concatenate(joined, axis=0)
        at = 0
        for i in members:
            rows = messages[i][1].shape[0]
            spots[i] = (len(wholes), at, rows)
            at += rows
        wholes.append(whole if way == "stay" else move(way, whole))
    return wholes, spots


def gather8(block):
    rows = block.shape[0]
    half = rows // 2
    arrays = [block]
    above, below = block, block
    for _ in range(3):
        above, below = [part.array for part in (yield [up(above), down(below)])]
        arrays += [above, below]
    arrays += [part.array for part in (yield [up(above[:half]), down(below[half:])])]
    pieces = [(0, 0, rows, 0, 0), (7, 0, half, 4, 0), (8, 0, half, 4, half)]
    for step in (1, 2, 3):
        pieces += [(2 * step - 1, 0, rows, step, 0), (2 * step, 0, rows, 8 - step, 0)]
    return arrays, pieces


def gather16(a, b):
    rows = a.shape[0]
    half = rows // 2
    join = functools.partial(jnp.concatenate, axis=0)
    first = yield [up(b), down(b), cross(a)]
    up1, down1, other_a = [part.array for part in first]
    second = yield [up(join([a, other_a, up1])), down(join([other_a, a, down1])), cross(join([b, up1, down1]))]
    up2, down2 = second[0].array, second[1].array
    third = yield [up(up2), down(down2), cross(join([up2[2 * rows :], down2[2 * rows :]]))]
    up3, down3 = third[0].array, third[1].array
    fourth = yield [
        up(up3[: 2 * rows + half]),
        down(join([down3[: 2 * rows], down3[2 * rows + half :]])),
        cross(join([up3[2 * rows :], down3[2 * rows :]])),
    ]
    up4, down4 = fourth[0].array, fourth[1].array
    fifth = yield [up(up4[:rows]), down(down4[:rows]), cross(join([up4[2 * rows :], down4[2 * rows :]]))]
    parts = [Part(a, 0, rows), Part(b, 0, rows), first[2], *first[:2], *second, *third, *fourth, *fifth]
    pieces = [(array, at + parts[array].first, *rest) for array, at, *rest in pieces_of(rows)]
    return [part.whole for part in parts], pieces


def pieces_of(rows):
    half = rows // 2
    pieces = [
        (0, 0, rows, 0, 0, 0),
        (1, 0, rows, 1, 0, 0),
        (2, 0, rows, 0, 8, 0),
        (3, 0, rows, 1, 1, 0),
        (4, 0, rows, 1, 7, 0),
        (7, 0, rows, 1, 8, 0),
        (7, rows, rows, 1, 9, 0),
        (7, 2 * rows, rows, 1, 15, 0),
        (10, 0, rows, 1, 10, 0),
        (10, rows, rows, 1, 14, 0),
        (13, 0, rows, 1, 11, 0),
        (13, rows, rows, 1, 13, 0),
        (14, 0, rows, 0, 4, 0),
        (15, 0, rows, 0, 12, 0),
        (16, 0, rows, 1, 12, 0),
        (11, 2 * rows, half, 1, 4, 0),
        (12, 2 * rows, half, 1, 4, half),
        (5, 2 * rows, rows, 1, 2, 0),
        (6, 2 * rows, rows, 1, 6, 0),
        (8, 2 * rows, rows, 1, 3, 0),
        (9, 2 * rows, rows, 1, 5, 0),
    ]
    for step, array in ((1, 5), (2, 8), (3, 11)):
        pieces += [(array, 0, rows, 0, step, 0), (array, rows, rows, 0, 8 + step, 0)]
    for step, array in ((1, 6), (2, 9), (3, 12)):
        pieces += [(array, 0, rows, 0, 16 - step, 0), (array, rows, rows, 0, 8 - step, 0)]
    return pieces


def rounds(*parts):
    results, left, live, back, now = [None] * len(parts), len(parts), {}, {}, 0
    while left:
        for i, (first, part) in enumerate(parts):
            if first == now:
                live[i] = part
        batch = {}
        for i in list(live):
            try:
                batch[i] = live[i].send(back.get(i))
            except StopIteration as end:
                results[i] = end.value
                left -= 1
                del live[i]
        wholes, spots = sent([message for group in batch.values() for message in group])
        wholes = lax.optimization_barrier(wholes)
        flat = [Part(wholes[which], first, rows) for which, first, rows in spots]
        for i, group in batch.items():
            back[i], flat = flat[: len(group)], flat[len(group) :]
        now += 1
    return results


ROW_TILE = 768


def project_kernel(pieces, first_col, split, place_ref, half_ref, db_hbm, *refs):
    count = 9
    w_refs = refs[:count]
    keep_k, keep_v, send_k, send_v, db_ref, w_ref, db_sem, w_sem = refs[count:]
    width = w_ref.shape[2] // 2
    copies = []
    for array, first, rows, place, at in pieces:
        block = w_ref.shape[1]
        for kind in range(2):
            low, high = max(at, kind * block), min(at + rows, (kind + 1) * block)
            if low < high:
                copies.append(
                    pltpu.make_async_copy(
                        w_refs[array].at[pl.ds(first + low - at, high - low), pl.ds(first_col, width)],
                        w_ref.at[place_ref[place], pl.ds(low - kind * block, high - low), pl.ds(kind * width, width)],
                        w_sem.at[len(copies)],
                    )
                )
                copies[-1].start()
    depth = w_ref.shape[0] * w_ref.shape[1]
    six = 2 * HELD
    turns = db_ref.shape[0] // 2 // (2 * six * 16)
    per_tile = ROW_TILE // (2 * six * 16)
    tiles = [(own, tile) for own in (0, 1) for tile in range(turns // per_tile)]
    loads = []
    for i, (own, tile) in enumerate(tiles):
        side = half_ref[0] if own else 1 - half_ref[0]
        start = pl.multiple_of(side * (turns * 2 * six * 16) + tile * ROW_TILE, ROW_TILE)
        loads.append(
            pltpu.make_async_copy(
                db_hbm.at[pl.ds(start, ROW_TILE)], db_ref.at[pl.ds(i * ROW_TILE, ROW_TILE)], db_sem.at[i]
            )
        )
        loads[-1].start()
    for copy in copies:
        copy.wait()
    for i, (own, tile) in enumerate(tiles):
        loads[i].wait()
        rows = db_ref[i * ROW_TILE : (i + 1) * ROW_TILE, :]
        part = jnp.dot(rows, w_ref[...].reshape(depth, 2 * width), preferred_element_type=F32)
        for j in range(ROW_TILE // 16):
            turn, entry = divmod(j, 2 * six)
            other, entry = divmod(entry, six)
            token = entry * TOK + (tile * per_tile + turn) * 16
            for kind, keep, send in ((0, keep_k, send_k), (1, keep_v, send_v)):
                at = token
                piece = part[j * 16 : (j + 1) * 16, kind * width : (kind + 1) * width]
                if split and kind == 0 and other:
                    at += (1 - own) * six * TOK
                    send[at : at + 16, :] = piece.astype(BF)
                elif split and kind == 0:
                    keep[1 - own, at : at + 16, :] = piece
                elif own:
                    keep[other, at : at + 16, :] = piece
                else:
                    at += other * six * TOK
                    send[at : at + 16, :] = piece.astype(BF)


def project(db, arrays, pieces, places, side, first_col, width, split):
    rows, depth = db.shape
    block = rows // 4
    vmem = pl.BlockSpec(memory_space=pltpu.VMEM)
    anywhere = pl.BlockSpec(memory_space=pl.ANY)
    smem = pl.BlockSpec(memory_space=pltpu.SMEM)
    return pl.pallas_call(
        functools.partial(project_kernel, pieces, first_col, split),
        out_shape=[jax.ShapeDtypeStruct((2, block, width), F32)] * 2 + [jax.ShapeDtypeStruct((2 * block, width), BF)] * 2,
        in_specs=[smem, smem] + [anywhere] * (1 + len(arrays)),
        out_specs=[vmem] * 4,
        scratch_shapes=[
            pltpu.VMEM((rows, depth), BF),
            pltpu.VMEM((ZN, depth // ZN, 2 * width), BF),
            pltpu.SemaphoreType.DMA((rows // ROW_TILE,)),
            pltpu.SemaphoreType.DMA((2 * len(pieces),)),
        ],
        compiler_params=pltpu.CompilerParams(vmem_limit_bytes=60 << 20),
        cost_estimate=pl.CostEstimate(flops=4 * rows * depth * width, bytes_accessed=12 << 20, transcendentals=0),
        name="project",
    )(places, side, db, *arrays)


TASKS = 32


def attend_kernel(pieces, first_col, layout, slot_ref, *refs):
    count = 17
    parts = sum(len(given) for given, _ in layout)
    outs = sum(len(made) for _, made in layout)
    q_refs, kv_refs, refs = refs[:parts], refs[parts : parts + count], refs[parts + count :]
    out_refs, stat_refs = refs[:outs], refs[outs : outs + len(layout)]
    q_ref, kv_ref, q_sem, sem = refs[outs + len(layout) :]
    width = kv_ref.shape[2]
    copies = []
    begin = 0
    for i, source in enumerate(q_refs):
        rows = source.shape[0]
        copies.append(
            pltpu.make_async_copy(source.at[:, pl.ds(first_col, width)], q_ref.at[pl.ds(begin, rows)], q_sem.at[i])
        )
        copies[-1].start()
        begin += rows
    for i, (array, first, rows, kind, place, at) in enumerate(pieces):
        copies.append(
            pltpu.make_async_copy(
                kv_refs[array].at[pl.ds(first, rows)],
                kv_ref.at[kind, pl.ds(place * 6 * TOK + at, rows)],
                sem.at[i],
            )
        )
        copies[-1].start()
    for copy in copies:
        copy.wait()
    lane = lax.broadcasted_iota(jnp.int32, (SEGMENT, 128), 1)
    heads = width // HDIM
    at_once = TASKS // heads

    def group(g, stat, segment, first, out_ref):
        tasks, scores, results = [], [], []
        for i in range(at_once):
            u = g * at_once + i
            at = pl.multiple_of(u * SEGMENT, SEGMENT)
            one = pl.multiple_of(slot_ref[2 * (segment + u)] * TOK, TOK)
            two = pl.multiple_of(slot_ref[2 * (segment + u) + 1] * TOK, TOK)
            for j in range(heads):
                tasks.append((first + u, at, one, two, j, slice(j * HDIM, (j + 1) * HDIM)))
        for u, at, one, two, j, cols in tasks:
            q = q_ref[pl.ds(segment * SEGMENT + at, SEGMENT), cols]
            keys = jnp.concatenate([kv_ref[0, pl.ds(one, TOK), cols], kv_ref[0, pl.ds(two, TOK), cols]], axis=0)
            score = lax.dot_general(q, keys, (((1,), (1,)), ((), ())), preferred_element_type=F32)
            scores.append(score * (HDIM**-0.5))
        tops = [jnp.max(score, axis=1, keepdims=True) for score in scores]
        weights = [jnp.exp(score - top) for score, top in zip(scores, tops)]
        for (u, at, one, two, j, cols), weight in zip(tasks, weights):
            values = jnp.concatenate([kv_ref[1, pl.ds(one, TOK), cols], kv_ref[1, pl.ds(two, TOK), cols]], axis=0)
            mixed = jnp.dot(weight.astype(BF), values, preferred_element_type=F32)
            results.append((mixed, jnp.sum(weight, axis=1, keepdims=True)))
        for (u, at, one, two, j, cols), (mixed, total), top in zip(tasks, results, tops):
            out_ref[pl.ds(at, SEGMENT), cols] = (mixed / total).astype(BF)
            stat = jnp.where(lane == u * heads + j, top + jnp.log(total), stat)
        return stat

    segment = 0
    out_refs = list(out_refs)
    for (_, made), stat_ref in zip(layout, stat_refs):
        first, stat = 0, jnp.zeros((SEGMENT, 128), F32)
        for rows in made:
            step = functools.partial(group, segment=segment, first=first, out_ref=out_refs.pop(0))
            stat = lax.fori_loop(0, rows // SEGMENT // at_once, step, stat)
            segment += rows // SEGMENT
            first += rows // SEGMENT
        stat_ref[...] = stat


def attend(sides, first_col, arrays, pieces):
    layout = [([part.shape[0] for part in parts], made) for _, parts, made in sides]
    queries = [part for _, parts, _ in sides for part in parts]
    slots = jnp.concatenate([slots for slots, _, _ in sides])
    outs = [rows for _, _, made in sides for rows in made]
    total = sum(outs)
    block, width = arrays[0].shape
    smem = pl.BlockSpec(memory_space=pltpu.SMEM)
    vmem = pl.BlockSpec(memory_space=pltpu.VMEM)
    anywhere = pl.BlockSpec(memory_space=pl.ANY)
    return pl.pallas_call(
        functools.partial(attend_kernel, pieces, first_col, layout),
        out_shape=[jax.ShapeDtypeStruct((rows, width), BF) for rows in outs]
        + [jax.ShapeDtypeStruct((SEGMENT, 128), F32)] * len(sides),
        in_specs=[smem] + [anywhere] * (len(queries) + len(arrays)),
        out_specs=[vmem] * (len(outs) + len(sides)),
        scratch_shapes=[
            pltpu.VMEM((total, width), BF),
            pltpu.VMEM((2, 16 * block, width), BF),
            pltpu.SemaphoreType.DMA((len(queries),)),
            pltpu.SemaphoreType.DMA((len(pieces),)),
        ],
        compiler_params=pltpu.CompilerParams(vmem_limit_bytes=60 << 20),
        cost_estimate=pl.CostEstimate(flops=4 * total * 128 * width, bytes_accessed=10 << 20, transcendentals=total * width),
        name="attend",
    )(slots, *queries, *arrays)


def merge_kernel(first_col, parts, mine_ref, stat_ref, other_ref, *refs):
    out_hbm, out_ref, sem = refs[-3:]
    lane = lax.broadcasted_iota(jnp.int32, (SEGMENT, 128), 1)
    width = mine_ref.shape[1]
    heads = width // HDIM
    difference = other_ref[...] - stat_ref[...]

    def unit(u, carry, first, theirs_ref):
        at = pl.multiple_of((first + u) * SEGMENT, SEGMENT)
        there = pl.multiple_of(u * SEGMENT, SEGMENT)
        for j in range(heads):
            cols = slice(j * HDIM, (j + 1) * HDIM)
            gap = jnp.sum(jnp.where(lane == (first + u) * heads + j, difference, 0.0), axis=1, keepdims=True)
            small = jnp.exp(-jnp.abs(gap))
            larger = 1.0 / (1.0 + small)
            smaller = small * larger
            share = jnp.where(gap > 0, smaller, larger)
            rest = jnp.where(gap > 0, larger, smaller)
            a = mine_ref[pl.ds(at, SEGMENT), cols].astype(F32)
            b = theirs_ref[pl.ds(there, SEGMENT), cols].astype(F32)
            out_ref[pl.ds(at, SEGMENT), cols] = (a * share + b * rest).astype(BF)
        return carry

    first = 0
    for theirs_ref in refs[:parts]:
        segments = theirs_ref.shape[0] // SEGMENT
        lax.fori_loop(0, segments, functools.partial(unit, first=first, theirs_ref=theirs_ref), 0, unroll=8)
        first += segments
    copy = pltpu.make_async_copy(out_ref, out_hbm.at[:, pl.ds(first_col, width)], sem)
    copy.start()
    copy.wait()


def merge(mine, theirs, stat, other, first_col, columns, so_far):
    rows, width = mine.shape
    vmem = pl.BlockSpec(memory_space=pltpu.VMEM)
    anywhere = pl.BlockSpec(memory_space=pl.ANY)
    extra = [] if so_far is None else [so_far]
    return pl.pallas_call(
        functools.partial(merge_kernel, first_col, len(theirs)),
        out_shape=jax.ShapeDtypeStruct((rows, columns), BF),
        in_specs=[vmem] * (3 + len(theirs)) + [anywhere] * len(extra),
        out_specs=anywhere,
        scratch_shapes=[pltpu.VMEM((rows, width), BF), pltpu.SemaphoreType.DMA],
        input_output_aliases={3 + len(theirs): 0} if extra else {},
        compiler_params=pltpu.CompilerParams(vmem_limit_bytes=24 << 20),
        cost_estimate=pl.CostEstimate(flops=8 * rows * width, bytes_accessed=6 * rows * width, transcendentals=rows),
        name="merge",
    )(mine, stat, other, *theirs, *extra)


def local(db_states, w_key, w_value, queries, nbr_owner, nbr_row):
    place = lax.axis_index("dp")
    x, z = place // ZN, place % ZN
    side = ((x + 1) // 2) % 2
    quarter = db_states.shape[2] // XN
    rows, columns = queries.shape

    def quarter_of(which):
        return lax.dynamic_slice_in_dim(db_states, which * quarter, quarter, axis=2)

    def database():
        arrived = yield [pair(quarter_of(x ^ 1)), cross(quarter_of(x ^ 3)), diagonal(quarter_of(x ^ 2))]
        by_pair, by_cross, by_diagonal = [part.array for part in arrived]
        own, even = quarter_of(x), x % 2 == 0
        order = [
            jnp.where(even, own, by_pair),
            jnp.where(even, by_pair, own),
            jnp.where(even, by_diagonal, by_cross),
            jnp.where(even, by_cross, by_diagonal),
        ]
        twelve = jnp.concatenate(order, axis=0)
        return lax.all_gather(twelve, "mp", axis=0, tiled=False).reshape(-1, quarter)

    def query_part(first, last):
        return pair(queries[first * rows // 16 : last * rows // 16])

    def early_queries():
        parts = yield [query_part(0, 5)]
        parts += yield [query_part(5, 10)]
        last, tables = yield [query_part(10, 13), pair(jnp.concatenate([nbr_owner, nbr_row], axis=1))]
        return [part.array for part in (*parts, last)], tables.array

    (w_arrays, w_pieces), db, (their_parts, tables) = rounds(
        (0, gather8(jnp.concatenate([w_key, w_value], axis=0))), (0, database()), (1, early_queries())
    )

    places = ((z - jnp.arange(ZN)) % ZN).astype(jnp.int32)
    flag = side.reshape(1).astype(jnp.int32)

    def slots(owner, row):
        from_x, from_z = owner // ZN, owner % ZN
        block = jnp.where(from_x // 2 == x // 2, 0, ZN) + (z - from_z) % ZN
        return (block * (2 * HELD) + (from_x % 2) * HELD + row).reshape(-1).astype(jnp.int32)

    own_slots = slots(nbr_owner, nbr_row)
    their_slots = slots(tables[:, :2], tables[:, 2:])

    shares = [
        project(db, w_arrays, w_pieces, places, flag, first * HDIM, heads * HDIM, first == 0) for first, heads in CHUNKS
    ]

    def plus(kept, *got):
        return sum([part.astype(F32) for part in got], kept).astype(BF)

    def summed_both_ways(share):
        keep_k, keep_v, send_k, send_v = share
        got_k, got_v = [part.array for part in (yield [cross(send_k), pair(send_v)])]
        half = send_k.shape[0] // 2
        last_k, last_v = yield [pair(plus(keep_k[1], got_k[half:])), cross(plus(keep_v[1], got_v[half:]))]
        return plus(keep_k[0], got_k[:half], last_k.array), plus(keep_v[0], got_v[:half], last_v.array)

    def summed_pair_first(share):
        keep_k, keep_v, send_k, send_v = share
        half = send_k.shape[0] // 2
        (got_v,) = [part.array for part in (yield [pair(send_v)])]
        got_k, last_v = [part.array for part in (yield [pair(send_k), cross(plus(keep_v[1], got_v[half:]))])]
        (last_k,) = yield [cross(plus(keep_k[1], got_k[half:]))]
        return plus(keep_k[0], got_k[:half], last_k.array), plus(keep_v[0], got_v[:half], last_v)

    found = {}

    def first_chunk():
        keys, values = yield from summed_both_ways(shares[0])
        found[0] = yield from gather16(keys, values)

    def second_chunk():
        yield [stay(array) for array in shares[1]]
        yield []
        yield []
        keys, values = yield from summed_pair_first(shares[1])
        found[1] = yield from gather16(keys, values)

    def last_queries():
        their_parts.extend(part.array for part in (yield [query_part(13, 16)]))

    results = []

    def answers():
        sides = [(their_slots, their_parts, [rows // 2, rows // 2]), (own_slots, [queries], [rows])]
        made = attend(sides, CHUNKS[0][0] * HDIM, *found[0])
        upper, *made = made
        lower, mine, stat, own_stat = [part.array for part in (yield [stay(array) for array in made])]
        upper, other = [part.array for part in (yield [pair(upper), pair(stat)])]
        (lower,) = [part.array for part in (yield [pair(lower)])]
        results.append((mine, [upper, lower], own_stat, other))

    rounds((0, first_chunk()), (0, second_chunk()), (6, last_queries()), (7, answers()))
    first_col = CHUNKS[1][0] * HDIM
    given, stat = attend([(their_slots, their_parts, [rows])], first_col, *found[1])
    theirs, other = move("pair", given), move("pair", stat)
    output = merge(*results[0], CHUNKS[0][0] * HDIM, columns, None)
    mine, own_stat = attend([(own_slots, [queries], [rows])], first_col, *found[1])
    return merge(mine, [theirs], own_stat, other, first_col, columns, output)


def solution(mesh):
    in_specs = (
        P("dp", "mp", None),
        P("dp", "mp"),
        P("dp", "mp"),
        P("dp", "mp"),
        P("dp", None),
        P("dp", None),
    )
    out_specs = P("dp", "mp")
    return jax.shard_map(local, mesh=mesh, in_specs=in_specs, out_specs=out_specs, check_vma=False)
```
